32 devices in a mesh: row: 4 (over x, core), col: 2 (over y), pair: 4 (over z).
Axes of the slice: x: 2, y: 2, z: 4, core: 2. Of those that a mesh axis runs over, the one named last changes fastest.
Arguments:
- frames: bfloat16 [4, 2, 64, 64, 256], P('pair', None, 'row', 'col'), may hold values from -6 to 6
- offsets: int32 [4, 2, 2, 2], P('pair'), may hold values from -8 to 8, as said below
- weight: bfloat16 [3, 3, 256, 256], replicated, may hold values from -0.125 to 0.125
- bias: float32 [256], replicated, may hold values from -3 to 3
- cotangent: bfloat16 [4, 81, 64, 64], P('pair', None, 'row', 'col'), may hold values from -0.023925781 to 0.023925781
Outputs:
- corr: bfloat16 [4, 81, 64, 64], P('pair', None, 'row', 'col')
- grad_weight: float32 [3, 3, 256, 256], replicated
- grad_bias: float32 [256], replicated
The draws below stay inside these ranges and needn't reach their ends.
Inputs may be any that keep to these rules, and one draw needn't show every extreme that they name: `offsets`: entry [.., 0] shifts rows and [.., 1] columns of one 32 x 32 block; both ends of the range occur in every draw.
All inputs are finite; a program needn't handle non-finite values.
Results may differ from the reference program's by a relative error of at most 0.0046.
Values may be sent and summed in bfloat16 or wider, within the bound.
A program may use at most 64 MiB of HBM per device.

```python
import jax
import jax.numpy as jnp
from jax import lax

CH = 256
BLK = 32
RAD = 4
MAXOFF = 8
DISP = 81
PAIRS = 4
H = 64
WD = 64


def draw_offsets(key, part):
    key_values = jax.random.fold_in(key, 11)
    key_first = jax.random.fold_in(key, 23)
    key_second = jax.random.fold_in(key, 37)
    blocks = H // BLK * (WD // BLK)
    drawn = jax.random.randint(key_values, (PAIRS, blocks, 2), -MAXOFF, MAXOFF + 1, dtype=jnp.int32)
    first_spot = jax.random.randint(key_first, (), 0, blocks, dtype=jnp.int32)
    second_spot = (first_spot + 1 + jax.random.randint(key_second, (), 0, blocks - 1, dtype=jnp.int32)) % blocks
    drawn = drawn.at[0, first_spot].set(jnp.array([-MAXOFF, MAXOFF], dtype=jnp.int32))
    drawn = drawn.at[0, second_spot].set(jnp.array([MAXOFF, -MAXOFF], dtype=jnp.int32))
    return drawn.reshape(PAIRS, H // BLK, WD // BLK, 2)


def steps_of(stream_key, dims, cuts, least, high):
    def one(dim, parts):
        steps = jax.random.uniform(jax.random.fold_in(jax.random.fold_in(stream_key, 6), dim), (parts,), jnp.float32, least / len(cuts), high / len(cuts))
        return jnp.repeat(jnp.exp(steps), dims[dim] // parts).reshape((-1,) + (1,) * (len(dims) - dim - 1))

    loudness = one(*cuts[0])
    for cut in cuts[1:]:
        loudness = loudness * one(*cut)
    return loudness


def scatter_about(own_key, extent, scale, most, split=(), held_as=jnp.bfloat16):
    entries = scale * jax.random.normal(own_key, extent, jnp.float32)
    if split:
        entries = entries * steps_of(own_key, extent, split, -0.22, 0.18)
    return jnp.clip(entries, -most, most).astype(held_as)


def setup_inputs(seed: int = 0) -> dict:
    seeds = jax.random.split(jax.random.key(seed), 6)
    return {
        "frames": scatter_about(seeds[0], (PAIRS, 2, H, WD, CH), 1.0, 6.0, ((0, 4), (2, 4), (3, 2))),
        "offsets": draw_offsets(jax.random.fold_in(seeds[5], 71), 0),
        "weight": scatter_about(seeds[2], (3, 3, CH, CH), (9 * CH) ** -0.5, 0.125),
        "bias": scatter_about(seeds[3], (CH,), 0.5, 3.0, (), jnp.float32),
        "cotangent": scatter_about(seeds[4], (PAIRS, DISP, H, WD), 0.004, 0.023925781, ((0, 4), (2, 4), (3, 2))),
    }


def band_take(scores):
    row_count, col_count, patch_width = scores.shape
    widened = jnp.pad(scores, ((0, 0), (0, 0), (0, 1)))
    flattened = widened.reshape(row_count, col_count * (patch_width + 1))
    flattened = jnp.pad(flattened, ((0, 0), (0, col_count)))
    return flattened.reshape(row_count, col_count, patch_width + 2)[:, :, :2 * RAD + 1]


def band_spread(bands, patch_width):
    row_count, col_count, window_size = bands.shape
    widened = jnp.pad(bands, ((0, 0), (0, 0), (0, patch_width + 2 - window_size)))
    flattened = widened.reshape(row_count, col_count * (patch_width + 2))[:, :col_count * (patch_width + 1)]
    return flattened.reshape(row_count, col_count, patch_width + 1)[:, :, :patch_width]


def block_scores(block_one, window_two):
    row_count, col_count = block_one.shape[0], block_one.shape[1]
    window_size = 2 * RAD + 1
    score_list = []
    for row_shift in range(window_size):
        scores = jnp.einsum("yxc,yzc->yxz", block_one.astype(jnp.float32), window_two[row_shift:row_shift + row_count].astype(jnp.float32), precision=lax.Precision.HIGHEST)
        score_list.append(band_take(scores))
    stacked = jnp.stack(score_list)
    return jnp.transpose(stacked, (0, 3, 1, 2)).reshape(window_size * window_size, row_count, col_count)


def block_grads(cot_block, block_one, window_two):
    row_count, col_count, channels = block_one.shape
    window_size = 2 * RAD + 1
    patch_width = col_count + 2 * RAD
    cot_grid = jnp.transpose(cot_block.reshape(window_size, window_size, row_count, col_count), (0, 2, 3, 1))
    grad_block = jnp.zeros((row_count, col_count, channels), jnp.float32)
    grad_window = jnp.zeros((row_count + 2 * RAD, patch_width, channels), jnp.float32)
    for row_shift in range(window_size):
        spread = band_spread(cot_grid[row_shift], patch_width).astype(jnp.float32)
        grad_block = grad_block + jnp.einsum("yxz,yzc->yxc", spread, window_two[row_shift:row_shift + row_count].astype(jnp.float32), precision=lax.Precision.HIGHEST)
        patch_term = jnp.einsum("yxz,yxc->yzc", spread, block_one.astype(jnp.float32), precision=lax.Precision.HIGHEST)
        grad_window = grad_window.at[row_shift:row_shift + row_count].add(patch_term)
    return grad_block, grad_window


def encode(image, weight, bias):
    conv_out = lax.conv_general_dilated(image[None], weight, (1, 1), "SAME", dimension_numbers=("NHWC", "HWIO", "NHWC"), preferred_element_type=jnp.float32)[0]
    return conv_out + bias


def weight_terms(image, delta):
    padded = jnp.pad(image, ((1, 1), (1, 1), (0, 0))).astype(jnp.float32)
    tap_list = []
    for tap_row in range(3):
        for tap_col in range(3):
            window = padded[tap_row:tap_row + H, tap_col:tap_col + WD]
            tap_list.append(jnp.einsum("yxc,yxd->cd", window, delta.astype(jnp.float32), precision=lax.Precision.HIGHEST))
    return jnp.stack(tap_list).reshape(3, 3, CH, CH)


def per_pair(inputs, weight, bias):
    frames_one, offsets_one, cotangent_first = inputs
    pre_one = encode(frames_one[0], weight, bias)
    pre_two = encode(frames_one[1], weight, bias)
    feat_one = jnp.maximum(pre_one, 0.0).astype(jnp.bfloat16)
    feat_two = jnp.maximum(pre_two, 0.0).astype(jnp.bfloat16)
    border_width = MAXOFF + RAD
    padded_two = jnp.pad(feat_two, ((border_width, border_width), (border_width, border_width), (0, 0)))
    block_cols = WD // BLK
    inv_root = CH ** -0.5

    def block_step(carried, block_index):
        grad_one, grad_two = carried
        block_row = block_index // block_cols
        block_col = block_index % block_cols
        shift_row = offsets_one[block_row, block_col, 0].astype(jnp.int32)
        shift_col = offsets_one[block_row, block_col, 1].astype(jnp.int32)
        block_top = (block_row * BLK).astype(jnp.int32)
        block_left = (block_col * BLK).astype(jnp.int32)
        zero_index = jnp.zeros((), jnp.int32)
        block_one = lax.dynamic_slice(feat_one, (block_top, block_left, zero_index), (BLK, BLK, CH))
        start = (block_top + shift_row + MAXOFF, block_left + shift_col + MAXOFF, zero_index)
        window_two = lax.dynamic_slice(padded_two, start, (BLK + 2 * RAD, BLK + 2 * RAD, CH))
        scores = block_scores(block_one, window_two) * inv_root
        cot_block = lax.dynamic_slice(cotangent_first, (zero_index, block_top, block_left), (DISP, BLK, BLK))
        grad_block, grad_window = block_grads(cot_block, block_one, window_two)
        grad_one = lax.dynamic_update_slice(grad_one, grad_block * inv_root, (block_top, block_left, zero_index))
        previous = lax.dynamic_slice(grad_two, start, grad_window.shape)
        grad_two = lax.dynamic_update_slice(grad_two, previous + grad_window * inv_root, start)
        return (grad_one, grad_two), scores.astype(jnp.bfloat16)

    carried = (jnp.zeros((H, WD, CH), jnp.float32), jnp.zeros((H + 2 * border_width, WD + 2 * border_width, CH), jnp.float32))
    blocks_all = (H // BLK) * block_cols
    (grad_one, gradient_second_padded), corr_blocks = lax.scan(block_step, carried, jnp.arange(blocks_all, dtype=jnp.int32))
    corr_one = jnp.transpose(corr_blocks.reshape(H // BLK, block_cols, DISP, BLK, BLK), (2, 0, 3, 1, 4)).reshape(DISP, H, WD)
    grad_two = gradient_second_padded[border_width:border_width + H, border_width:border_width + WD]
    delta_one = jnp.where(pre_one > 0, grad_one, 0.0).astype(jnp.bfloat16)
    delta_two = jnp.where(pre_two > 0, grad_two, 0.0)
    grad_w = weight_terms(frames_one[0], delta_one) + weight_terms(frames_one[1], delta_two)
    grad_b = jnp.sum(delta_one.astype(jnp.float32), axis=(0, 1)) + jnp.sum(delta_two, axis=(0, 1))
    return corr_one, grad_w, grad_b


def reference(frames, offsets, weight, bias, cotangent):
    corr, grad_w, grad_b = lax.map(lambda inputs: per_pair(inputs, weight, bias), (frames, offsets, cotangent))
    return corr, jnp.sum(grad_w, axis=0), jnp.sum(grad_b, axis=0)
```

```python
import functools

import jax
import jax.numpy as jnp
from jax import lax
from jax.experimental import pallas as pl
from jax.experimental.pallas import tpu as pltpu
from jax.sharding import PartitionSpec as P

BLK = 32
RAD = 4
MAXOFF = 8
MESH = pl.DeviceIdType.MESH


def with_halo(cells, sides, width):
    for axis, dim in sides:
        count = lax.axis_size(axis)
        ends = count - 1
        head = lax.slice_in_dim(cells, 0, width, axis=dim)
        tail = lax.slice_in_dim(cells, cells.shape[dim] - width, cells.shape[dim], axis=dim)
        cells = jnp.concatenate(
            [
                lax.ppermute(tail, axis, [(i, (i + 1) % count) for i in range(ends)]),
                cells,
                lax.ppermute(head, axis, [((i + 1) % count, i) for i in range(ends)]),
            ],
            axis=dim,
        )
    return cells


def band_take(scores):
    row_count, col_count, patch_width = scores.shape
    widened = jnp.pad(scores, ((0, 0), (0, 0), (0, 1)))
    flattened = widened.reshape(row_count, col_count * (patch_width + 1))
    flattened = jnp.pad(flattened, ((0, 0), (0, col_count)))
    return flattened.reshape(row_count, col_count, patch_width + 2)[:, :, : 2 * RAD + 1]


def band_spread(bands, patch_width):
    row_count, col_count, window_size = bands.shape
    widened = jnp.pad(bands, ((0, 0), (0, 0), (0, patch_width + 2 - window_size)))
    flattened = widened.reshape(row_count, col_count * (patch_width + 2))[
        :, : col_count * (patch_width + 1)
    ]
    return flattened.reshape(row_count, col_count, patch_width + 1)[:, :, :patch_width]


def block_scores(block_one, window_two):
    row_count, col_count = (block_one.shape[0], block_one.shape[1])
    window_size = 2 * RAD + 1
    score_list = []
    for row_shift in range(window_size):
        scores = jnp.einsum(
            "yxc,yzc->yxz",
            block_one,
            window_two[row_shift : row_shift + row_count],
            preferred_element_type=jnp.float32,
        )
        score_list.append(band_take(scores))
    stacked = jnp.stack(score_list)
    return jnp.transpose(stacked, (0, 3, 1, 2)).reshape(
        window_size * window_size, row_count, col_count
    )


def block_grads(cot_block, block_one, window_two):
    row_count, col_count, channels = block_one.shape
    window_size = 2 * RAD + 1
    patch_width = col_count + 2 * RAD
    cot_grid = jnp.transpose(
        cot_block.reshape(window_size, window_size, row_count, col_count), (0, 2, 3, 1)
    )
    grad_block = jnp.zeros((row_count, col_count, channels), jnp.float32)
    grad_window = jnp.zeros((row_count + 2 * RAD, patch_width, channels), jnp.float32)
    for row_shift in range(window_size):
        spread = band_spread(cot_grid[row_shift], patch_width)
        grad_block = grad_block + jnp.einsum(
            "yxz,yzc->yxc",
            spread,
            window_two[row_shift : row_shift + row_count],
            preferred_element_type=jnp.float32,
        )
        patch_term = jnp.einsum(
            "yxz,yxc->yzc", spread, block_one, preferred_element_type=jnp.float32
        )
        grad_window = grad_window.at[row_shift : row_shift + row_count].add(patch_term)
    return (grad_block, grad_window)


def convolve(padded, weight, bias, row_count, col_count):
    channels = weight.shape[3]
    accumulated = jnp.zeros((row_count * col_count, channels), jnp.float32)
    for tap_row in range(3):
        for tap_col in range(3):
            window = padded[tap_row : tap_row + row_count, tap_col : tap_col + col_count].reshape(
                row_count * col_count, -1
            )
            accumulated = accumulated + jnp.dot(
                window, weight[tap_row, tap_col], preferred_element_type=jnp.float32
            )
    return accumulated.reshape(row_count, col_count, channels) + bias


def weight_terms(padded, delta, input_float):
    row_count, col_count, channels = delta.shape
    flat_delta = delta.reshape(row_count * col_count, channels)
    tap_list = []
    for tap_row in range(3):
        for tap_col in range(3):
            window = padded[tap_row : tap_row + row_count, tap_col : tap_col + col_count].reshape(
                row_count * col_count, -1
            )
            if input_float:
                tap_list.append(
                    jnp.einsum(
                        "pc,pd->cd",
                        window.astype(jnp.float32),
                        flat_delta,
                        precision=lax.Precision.HIGHEST,
                    )
                )
            else:
                tap_list.append(
                    jnp.einsum("pc,pd->cd", window, flat_delta, preferred_element_type=jnp.float32)
                )
    return jnp.stack(tap_list).reshape(3, 3, channels, channels)


def exchange_plan():
    sizes = {axis: lax.axis_size(axis) for axis in ("row", "col", "pair")}
    bits = {
        axis: [1 << place for place in range(size.bit_length() - 1)]
        for axis, size in sizes.items()
    }
    near = [("row", stride) for stride in bits["row"][:1]]
    rest = [("row", stride) for stride in bits["row"][1:]]
    side = [("col", stride) for stride in reversed(bits["col"])]
    deep = [("pair", stride) for stride in reversed(bits["pair"])]
    return [near + rest + side + deep, near + side + rest + deep]


def sum_kernel(plans, terms, total, acc, send_half, recv_half, recv_wide, *sems):
    rs_send, rs_recv, ag_send, ag_recv = sems
    rows = terms.shape[1]
    count = len(plans[0])
    parts = range(len(plans))

    def partner(step):
        axis, stride = step
        me = lax.axis_index(axis)
        bit = lax.rem(me // stride, 2)
        return bit, {axis: me + stride - 2 * stride * bit}

    barrier = pltpu.get_barrier_semaphore()
    for step in plans[0]:
        pl.semaphore_signal(barrier, inc=1, device_id=partner(step)[1], device_id_type=MESH)
    pl.semaphore_wait(barrier, count)

    base = [0 for _ in parts]
    trail = [[] for _ in parts]
    waiting = [None for _ in parts]
    sent = []

    def absorb(part, place):
        size = rows >> (place + 1)
        copy, keep, came, wide = waiting[part]
        copy.wait_recv()
        source = terms if place == 0 else acc
        add = came[...] if wide else came[...].astype(jnp.float32)
        acc[part, pl.ds(keep, size), :] = source[part, pl.ds(keep, size), :] + add
        base[part] = keep

    for place in range(count):
        size = rows >> (place + 1)
        slot = rows - (rows >> place)
        wide = place == 0 or place == count - 1
        for part in parts:
            if place > 0:
                absorb(part, place - 1)
            bit, device = partner(plans[part][place])
            keep = pl.multiple_of(base[part] + bit * size, 16)
            give = pl.multiple_of(base[part] + (1 - bit) * size, 16)
            if wide:
                source = terms if place == 0 else acc
                first = 0 if place == 0 else rows // 2
                src = source.at[part, pl.ds(give, size), :]
                dst = recv_wide.at[part, pl.ds(first, size), :]
            else:
                send_half[part, slot : slot + size, :] = acc[part, pl.ds(give, size), :].astype(
                    jnp.bfloat16
                )
                src = send_half.at[part, pl.ds(slot, size), :]
                dst = recv_half.at[part, pl.ds(slot, size), :]
            copy = pltpu.make_async_remote_copy(
                src_ref=src,
                dst_ref=dst,
                send_sem=rs_send.at[part, place],
                recv_sem=rs_recv.at[part, place],
                device_id=device,
                device_id_type=MESH,
            )
            copy.start()
            sent.append(copy)
            waiting[part] = (copy, keep, dst, wide)
            trail[part].append(base[part])
    for part in parts:
        absorb(part, count - 1)
        size = rows >> count
        own = pl.multiple_of(base[part], 16)
        total[part, pl.ds(own, size), :] = acc[part, pl.ds(own, size), :].astype(jnp.bfloat16)
    for place in reversed(range(count)):
        size = rows >> (place + 1)
        for part in parts:
            if place < count - 1:
                waiting[part].wait_recv()
            block = total.at[part, pl.ds(pl.multiple_of(base[part], 16), size), :]
            copy = pltpu.make_async_remote_copy(
                src_ref=block,
                dst_ref=block,
                send_sem=ag_send.at[part, place],
                recv_sem=ag_recv.at[part, place],
                device_id=partner(plans[part][place])[1],
                device_id_type=MESH,
            )
            copy.start()
            sent.append(copy)
            waiting[part] = copy
            base[part] = trail[part][place]
    for part in parts:
        waiting[part].wait_recv()
    for copy in sent:
        copy.wait_send()


def padded_rows(rows):
    devices = lax.axis_size("row") * lax.axis_size("col") * lax.axis_size("pair")
    grain = 16 * devices
    return (rows + grain - 1) // grain * grain


def sum_everywhere(terms):
    plans = exchange_plan()
    parts, rows, lanes = terms.shape
    count = len(plans[0])
    semaphores = pltpu.SemaphoreType.DMA((parts, count))
    return pl.pallas_call(
        functools.partial(sum_kernel, plans),
        out_shape=jax.ShapeDtypeStruct(terms.shape, jnp.bfloat16),
        in_specs=[pl.BlockSpec(memory_space=pltpu.VMEM)],
        out_specs=pl.BlockSpec(memory_space=pltpu.VMEM),
        scratch_shapes=[
            pltpu.VMEM(terms.shape, jnp.float32),
            pltpu.VMEM(terms.shape, jnp.bfloat16),
            pltpu.VMEM(terms.shape, jnp.bfloat16),
            pltpu.VMEM(terms.shape, jnp.float32),
            semaphores,
            semaphores,
            semaphores,
            semaphores,
        ],
        compiler_params=pltpu.CompilerParams(
            collective_id=1, has_side_effects=True, vmem_limit_bytes=32 * 2**20
        ),
        name="sum_everywhere",
    )(terms)


def shards(frames, offsets, weight, bias, cotangent):
    tile_rows, tile_cols, channels = (frames.shape[2], frames.shape[3], frames.shape[4])
    border_width = MAXOFF + RAD
    row_start = lax.axis_index("row") * tile_rows
    col_start = lax.axis_index("col") * tile_cols
    inv_root = channels ** (-0.5)
    bordered = with_halo(frames, (("row", 2), ("col", 3)), 1)
    first_pad = bordered[0, 0]
    second_pad = bordered[0, 1]
    pre_one = convolve(first_pad, weight, bias, tile_rows, tile_cols)
    pre_two = convolve(second_pad, weight, bias, tile_rows, tile_cols)
    feat_two = jnp.maximum(pre_two, 0.0).astype(jnp.bfloat16)
    padded_two = with_halo(feat_two, (("row", 0), ("col", 1)), border_width)
    feat_one = jnp.maximum(pre_one, 0.0).astype(jnp.bfloat16)
    sub_rows = min(tile_rows, BLK)
    gradient_second_padded = jnp.zeros(
        (tile_rows + 2 * border_width, tile_cols + 2 * border_width, channels), jnp.float32
    )
    zero_index = jnp.zeros((), jnp.int32)
    block_row = (row_start + 0) // BLK
    block_col = (col_start + 0) // BLK
    shift_pair = offsets[0, block_row, block_col]
    start = (0 + shift_pair[0] + MAXOFF, 0 + shift_pair[1] + MAXOFF, zero_index)
    window_two = lax.dynamic_slice(padded_two, start, (sub_rows + 2 * RAD, BLK + 2 * RAD, channels))
    corr_pieces = block_scores(feat_one, window_two) * inv_root
    cot_block = cotangent[0, :, 0:sub_rows, 0:BLK]
    grad_block, grad_window = block_grads(cot_block, feat_one, window_two)
    grad_pieces = grad_block * inv_root
    gradient_second_padded = lax.dynamic_update_slice(
        gradient_second_padded, grad_window * inv_root, start
    )
    corr = corr_pieces.astype(jnp.bfloat16)[None]
    carried_state = jnp.concatenate(
        [gradient_second_padded[:border_width], gradient_second_padded[-border_width:]], axis=0
    )
    incoming_block = with_halo(
        carried_state.astype(jnp.bfloat16), (("row", 0),), border_width
    ).astype(carried_state.dtype)
    central_index = gradient_second_padded[border_width : border_width + tile_rows]
    central_index = central_index.at[:border_width].add(incoming_block[:border_width])
    central_index = central_index.at[tile_rows - border_width :].add(
        incoming_block[3 * border_width :]
    )
    carried_state = jnp.concatenate(
        [central_index[:, :border_width], central_index[:, -border_width:]], axis=1
    )
    incoming_block = with_halo(
        carried_state.astype(jnp.bfloat16), (("col", 1),), border_width
    ).astype(carried_state.dtype)
    center = central_index[:, border_width : border_width + tile_cols]
    center = center.at[:, :border_width].add(incoming_block[:, :border_width])
    center = center.at[:, tile_cols - border_width :].add(incoming_block[:, 3 * border_width :])
    delta_two = jnp.where(pre_two > 0, center, 0.0)
    delta_one = jnp.where(pre_one > 0, grad_pieces, 0.0).astype(jnp.bfloat16)
    grad_w = weight_terms(first_pad, delta_one, False) + weight_terms(second_pad, delta_two, True)
    grad_b = jnp.sum(delta_one.astype(jnp.float32), axis=(0, 1)) + jnp.sum(delta_two, axis=(0, 1))
    flat = jnp.concatenate([grad_w.reshape(-1, channels), grad_b[None]], axis=0)
    rows = flat.shape[0]
    flat = jnp.pad(flat, ((0, padded_rows(rows) - rows), (0, 0)))
    halves = jnp.stack([flat[:, : channels // 2], flat[:, channels // 2 :]])
    summed = sum_everywhere(halves).astype(jnp.float32)
    summed = jnp.concatenate([summed[0, :rows], summed[1, :rows]], axis=1)
    return (corr, summed[: rows - 1].reshape(grad_w.shape), summed[rows - 1])


def solution(mesh):
    return jax.shard_map(
        shards,
        mesh=mesh,
        in_specs=(
            P("pair", None, "row", "col", None),
            P("pair", None, None, None),
            P(),
            P(),
            P("pair", None, "row", "col"),
        ),
        out_specs=(P("pair", None, "row", "col"), P(), P()),
        check_vma=False,
    )
```

```python
import functools

import jax
import jax.numpy as jnp
from jax import lax
from jax.experimental import pallas as pl
from jax.experimental.pallas import tpu as pltpu
from jax.sharding import PartitionSpec as P

BLK = 32
RAD = 4
MAXOFF = 8
MESH = pl.DeviceIdType.MESH


def exchange_plan():
    sizes = {axis: lax.axis_size(axis) for axis in ("row", "col", "pair")}
    bits = {
        axis: [1 << place for place in range(size.bit_length() - 1)]
        for axis, size in sizes.items()
    }
    near = [("row", stride) for stride in bits["row"][:1]]
    rest = [("row", stride) for stride in bits["row"][1:]]
    side = [("col", stride) for stride in reversed(bits["col"])]
    deep = [("pair", stride) for stride in reversed(bits["pair"])]
    return [near + rest + side + deep, near + side + rest + deep]


def sum_kernel(plans, terms, total, acc, send_half, recv_half, recv_wide, *sems):
    rs_send, rs_recv, ag_send, ag_recv = sems
    rows = terms.shape[1]
    count = len(plans[0])
    parts = range(len(plans))

    def partner(step):
        axis, stride = step
        me = lax.axis_index(axis)
        bit = lax.rem(me // stride, 2)
        return bit, {axis: me + stride - 2 * stride * bit}

    barrier = pltpu.get_barrier_semaphore()
    for step in plans[0]:
        pl.semaphore_signal(barrier, inc=1, device_id=partner(step)[1], device_id_type=MESH)
    pl.semaphore_wait(barrier, count)

    base = [0 for _ in parts]
    trail = [[] for _ in parts]
    waiting = [None for _ in parts]
    sent = []

    def absorb(part, place):
        size = rows >> (place + 1)
        copy, keep, came, wide = waiting[part]
        copy.wait_recv()
        source = terms if place == 0 else acc
        add = came[...] if wide else came[...].astype(jnp.float32)
        acc[part, pl.ds(keep, size), :] = source[part, pl.ds(keep, size), :] + add
        base[part] = keep

    for place in range(count):
        size = rows >> (place + 1)
        slot = rows - (rows >> place)
        wide = place == 0 or place == count - 1
        for part in parts:
            if place > 0:
                absorb(part, place - 1)
            bit, device = partner(plans[part][place])
            keep = pl.multiple_of(base[part] + bit * size, 16)
            give = pl.multiple_of(base[part] + (1 - bit) * size, 16)
            if wide:
                source = terms if place == 0 else acc
                first = 0 if place == 0 else rows // 2
                src = source.at[part, pl.ds(give, size), :]
                dst = recv_wide.at[part, pl.ds(first, size), :]
            else:
                send_half[part, slot : slot + size, :] = acc[part, pl.ds(give, size), :].astype(
                    jnp.bfloat16
                )
                src = send_half.at[part, pl.ds(slot, size), :]
                dst = recv_half.at[part, pl.ds(slot, size), :]
            copy = pltpu.make_async_remote_copy(
                src_ref=src,
                dst_ref=dst,
                send_sem=rs_send.at[part, place],
                recv_sem=rs_recv.at[part, place],
                device_id=device,
                device_id_type=MESH,
            )
            copy.start()
            sent.append(copy)
            waiting[part] = (copy, keep, dst, wide)
            trail[part].append(base[part])
    for part in parts:
        absorb(part, count - 1)
        size = rows >> count
        own = pl.multiple_of(base[part], 16)
        total[part, pl.ds(own, size), :] = acc[part, pl.ds(own, size), :].astype(jnp.bfloat16)
    for place in reversed(range(count)):
        size = rows >> (place + 1)
        for part in parts:
            if place < count - 1:
                waiting[part].wait_recv()
            block = total.at[part, pl.ds(pl.multiple_of(base[part], 16), size), :]
            copy = pltpu.make_async_remote_copy(
                src_ref=block,
                dst_ref=block,
                send_sem=ag_send.at[part, place],
                recv_sem=ag_recv.at[part, place],
                device_id=partner(plans[part][place])[1],
                device_id_type=MESH,
            )
            copy.start()
            sent.append(copy)
            waiting[part] = copy
            base[part] = trail[part][place]
    for part in parts:
        waiting[part].wait_recv()
    for copy in sent:
        copy.wait_send()


def padded_rows(rows):
    devices = lax.axis_size("row") * lax.axis_size("col") * lax.axis_size("pair")
    grain = 16 * devices
    return (rows + grain - 1) // grain * grain


def sum_everywhere(terms):
    plans = exchange_plan()
    parts, rows, lanes = terms.shape
    count = len(plans[0])
    semaphores = pltpu.SemaphoreType.DMA((parts, count))
    return pl.pallas_call(
        functools.partial(sum_kernel, plans),
        out_shape=jax.ShapeDtypeStruct(terms.shape, jnp.bfloat16),
        in_specs=[pl.BlockSpec(memory_space=pltpu.VMEM)],
        out_specs=pl.BlockSpec(memory_space=pltpu.VMEM),
        scratch_shapes=[
            pltpu.VMEM(terms.shape, jnp.float32),
            pltpu.VMEM(terms.shape, jnp.bfloat16),
            pltpu.VMEM(terms.shape, jnp.bfloat16),
            pltpu.VMEM(terms.shape, jnp.float32),
            semaphores,
            semaphores,
            semaphores,
            semaphores,
        ],
        compiler_params=pltpu.CompilerParams(
            collective_id=1, has_side_effects=True, vmem_limit_bytes=32 * 2**20
        ),
        name="sum_everywhere",
    )(terms)


def halo_kernel(wide, edge, frames, pad_one, pad_two, send_sem, recv_sem, own_sem):
    row, col = lax.axis_index("row"), lax.axis_index("col")
    row_count, col_count = lax.axis_size("row"), lax.axis_size("col")
    tile_rows, tile_cols = frames.shape[1], frames.shape[2]
    ways = [(down, right) for down in (0, -1, 1) for right in (0, -1, 1) if (down, right) != (0, 0)]

    def lies(down, right):
        inside_rows = (row + down >= 0) & (row + down < row_count)
        inside_cols = (col + right >= 0) & (col + right < col_count)
        return inside_rows & inside_cols

    def device(down, right):
        return {"row": row + down, "col": col + right}

    def span(step, size, halo):
        if step == 0:
            return pl.ds(0, size), pl.ds(halo, size)
        if step > 0:
            return pl.ds(size - halo, halo), pl.ds(0, halo)
        return pl.ds(0, halo), pl.ds(halo + size, halo)

    barrier = pltpu.get_barrier_semaphore()
    for way in ways:
        @pl.when(lies(*way))
        def _():
            pl.semaphore_signal(barrier, inc=1, device_id=device(*way), device_id_type=MESH)
    own = []
    for frame, (pad, halo) in enumerate(((pad_one, 1), (pad_two, wide))):
        middle = pad.at[pl.ds(halo, tile_rows), pl.ds(edge, tile_cols), :]
        own.append(pltpu.make_async_copy(frames.at[frame], middle, own_sem.at[frame]))
        own[-1].start()
    near_rows = 1 + (row > 0).astype(jnp.int32) + (row < row_count - 1).astype(jnp.int32)
    near_cols = 1 + (col > 0).astype(jnp.int32) + (col < col_count - 1).astype(jnp.int32)
    pl.semaphore_wait(barrier, near_rows * near_cols - 1)
    copies = []
    for place, way in enumerate(ways):
        for frame, (pad, halo) in enumerate(((pad_one, 1), (pad_two, wide))):
            take_rows, put_rows = span(way[0], tile_rows, halo)
            take_cols, put_cols = span(way[1], tile_cols, edge)
            copy = pltpu.make_async_remote_copy(
                src_ref=frames.at[frame, take_rows, take_cols, :],
                dst_ref=pad.at[put_rows, put_cols, :],
                send_sem=send_sem.at[place, frame],
                recv_sem=recv_sem.at[place, frame],
                device_id=device(*way),
                device_id_type=MESH,
            )
            copies.append((way, copy))
            pl.when(lies(*way))(copy.start)
    for copy in own:
        copy.wait()
    for way, copy in copies:
        pl.when(lies(-way[0], -way[1]))(copy.wait_recv)
    for way, copy in copies:
        pl.when(lies(*way))(copy.wait_send)


def gather_halos(frames, wide, edge):
    tile_rows, tile_cols, channels = frames.shape[1:]
    pads = [
        jax.ShapeDtypeStruct((tile_rows + 2 * halo, tile_cols + 2 * edge, channels), frames.dtype)
        for halo in (1, wide)
    ]
    return pl.pallas_call(
        functools.partial(halo_kernel, wide, edge),
        out_shape=pads,
        in_specs=[pl.BlockSpec(memory_space=pl.ANY)],
        out_specs=[pl.BlockSpec(memory_space=pl.ANY)] * 2,
        scratch_shapes=[
            pltpu.SemaphoreType.DMA((8, 2)),
            pltpu.SemaphoreType.DMA((8, 2)),
            pltpu.SemaphoreType.DMA((2,)),
        ],
        compiler_params=pltpu.CompilerParams(collective_id=0, has_side_effects=True),
        name="gather_halos",
    )(frames)


def tile_kernel(
    geometry, place, pad_one, pad_two, weight, bias, cot, corr, terms,
    taps_one, taps_two, pre_one, pre_two, feat_one, feat_two, delta_one, flip_one, flip_two,
    grad_two, cot_wide, corr_wide, lanes_wide,
):
    tile_rows, tile_cols, image_rows, image_cols, edge, width = geometry
    channels = bias.shape[1]
    side = 2 * RAD + 1
    lanes = lanes_wide.shape[0]
    padded_cols = tile_cols + 2 * edge
    window_rows = tile_rows + 2 * RAD
    pixels_two = window_rows * width
    shift_row, shift_col, row_start, col_start = place[0], place[1], place[2], place[3]
    inv_root = channels ** (-0.5)

    across = lax.broadcasted_iota(jnp.int32, (padded_cols, channels), 0) + (col_start - edge)
    inside_cols = (across >= 0) & (across < image_cols)

    def masked(line, image_row):
        inside = inside_cols & (image_row >= 0) & (image_row < image_rows)
        return jnp.where(inside, line.astype(jnp.float32), 0.0)

    @pl.loop(0, tile_rows + 2)
    def _(line):
        cells = masked(pad_one[line], row_start - 1 + line)
        for tap in range(3):
            first = edge - 1 + tap
            taps_one[pl.ds(pl.multiple_of(line * tile_cols, 16), tile_cols),
                     tap * channels : (tap + 1) * channels] = (
                cells[first : first + tile_cols].astype(jnp.bfloat16)
            )

    @pl.loop(0, window_rows + 2)
    def _(line):
        at = shift_row + MAXOFF + line
        cells = masked(pad_two[at], row_start - (MAXOFF + RAD + 1) + at)
        cells = pltpu.roll(cells, padded_cols - (shift_col + edge - RAD - 1), 0)
        for tap in range(3):
            taps_two[pl.ds(pl.multiple_of(line * width, 16), width),
                     tap * channels : (tap + 1) * channels] = (
                cells[tap : tap + width].astype(jnp.bfloat16)
            )

    def convolved(taps, first, size, pitch):
        total = jnp.broadcast_to(bias[...], (size, channels))
        for tap in range(3):
            total = total + jnp.dot(
                taps[pl.ds(pl.multiple_of(first + tap * pitch, 16), size), :],
                weight[tap],
                preferred_element_type=jnp.float32,
            )
        return total

    group = 4
    size_one = group * tile_cols

    @pl.loop(0, tile_rows // group)
    def _(block):
        first = pl.multiple_of(block * size_one, 16)
        pre = convolved(taps_one, first, size_one, tile_cols)
        pre_one[pl.ds(first, size_one), :] = pre
        feat_one[pl.ds(first, size_one), :] = jnp.maximum(pre, 0.0).astype(jnp.bfloat16)

    size_two = group * width

    @pl.loop(0, window_rows // group)
    def _(block):
        first = pl.multiple_of(block * size_two, 16)
        pre = convolved(taps_two, first, size_two, width).reshape(group, width, channels)
        rows = lax.broadcasted_iota(jnp.int32, pre.shape, 0) + (
            row_start + shift_row - RAD + block * group
        )
        cols = lax.broadcasted_iota(jnp.int32, pre.shape, 1) + (col_start + shift_col - RAD)
        inside = (rows >= 0) & (rows < image_rows) & (cols >= 0) & (cols < image_cols)
        pre = jnp.where(inside, pre, 0.0).reshape(size_two, channels)
        pre_two[pl.ds(first, size_two), :] = pre
        feat_two[pl.ds(first, size_two), :] = jnp.maximum(pre, 0.0).astype(jnp.bfloat16)

    feat_two[pixels_two:, :] = jnp.zeros_like(feat_two[pixels_two:, :])
    grad_two[...] = jnp.zeros_like(grad_two)
    cot_wide[...] = cot[...].astype(jnp.float32)
    lanes_wide[...] = jnp.zeros_like(lanes_wide)

    def skew(cells, back):
        line = lax.rem(lax.broadcasted_iota(jnp.int32, cells.shape, 0), tile_cols)
        step = 1
        while step < tile_cols:
            moved = pltpu.roll(cells, lanes - step if back else step, 1)
            cells = jnp.where((line // step) % 2 == 1, moved, cells)
            step *= 2
        return cells

    @pl.loop(0, tile_rows // group)
    def _(block):
        at = pl.ds(pl.multiple_of(block * size_one, 128), size_one)
        for line in range(side):
            lanes_wide[line * width : line * width + side, :] = cot_wide[
                line * side : (line + 1) * side, at
            ]
        spread_all = skew(lanes_wide[...].T, False).astype(jnp.bfloat16)
        score_list = []
        for inner in range(group):
            row = block * group + inner
            spread = spread_all[inner * tile_cols : (inner + 1) * tile_cols]
            pixels = pl.ds(pl.multiple_of(row * tile_cols, 16), tile_cols)
            window = pl.ds(pl.multiple_of(row * width, 16), lanes)
            one, two = feat_one[pixels, :], feat_two[window, :]
            score_list.append(
                lax.dot_general(one, two, (((1,), (1,)), ((), ())), preferred_element_type=jnp.float32)
            )
            grad = jnp.dot(spread, two, preferred_element_type=jnp.float32) * inv_root
            grad = jnp.where(pre_one[pixels, :] > 0, grad, 0.0)
            delta_one[pixels, :] = grad.astype(jnp.bfloat16).astype(jnp.float32)
            grad_two[window, :] += lax.dot_general(
                spread, one, (((0,), (0,)), ((), ())), preferred_element_type=jnp.float32
            )
        scores = skew(jnp.concatenate(score_list, axis=0), True).T * inv_root
        for line in range(side):
            corr_wide[line * side : (line + 1) * side, at] = scores[
                line * width : line * width + side
            ]

    corr[...] = corr_wide[...].astype(jnp.bfloat16)
    delta_two = jnp.where(pre_two[...] > 0, grad_two[:pixels_two, :] * inv_root, 0.0)
    bias_term = jnp.sum(delta_one[...], axis=0, keepdims=True)
    bias_term = bias_term + jnp.sum(delta_two, axis=0, keepdims=True)
    flip_one[...] = delta_one[...].T.astype(jnp.bfloat16)
    flip_two[...] = delta_two.T.astype(jnp.bfloat16)

    half = channels // 2
    pixels_one = tile_rows * tile_cols
    for tap_row in range(3):
        for tap_col in range(3):
            cols = slice(tap_col * channels, (tap_col + 1) * channels)
            first_one, first_two = tap_row * tile_cols, tap_row * width
            term = jnp.dot(
                flip_one[...],
                taps_one[first_one : first_one + pixels_one, cols],
                preferred_element_type=jnp.float32,
            ) + jnp.dot(
                flip_two[...],
                taps_two[first_two : first_two + pixels_two, cols],
                preferred_element_type=jnp.float32,
            )
            term = term.T
            first = (tap_row * 3 + tap_col) * channels
            terms[0, first : first + channels, :] = term[:, :half]
            terms[1, first : first + channels, :] = term[:, half:]
    last = 9 * channels
    rest = terms.shape[1] - last
    filler = lax.broadcasted_iota(jnp.int32, (rest, channels), 0) == 0
    filler = jnp.where(filler, jnp.broadcast_to(bias_term, (rest, channels)), 0.0)
    terms[0, last:, :] = filler[:, :half]
    terms[1, last:, :] = filler[:, half:]


def spread_kernel(summed, grad_weight, grad_bias):
    rows, half = grad_weight.shape[0], summed.shape[2]
    for part in range(2):
        lanes = slice(part * half, (part + 1) * half)
        grad_weight[:, lanes] = summed[part, :rows, :].astype(jnp.float32)
        grad_bias[:, lanes] = summed[part, rows : rows + 16, :].astype(jnp.float32)[:1]


def shards(frames, offsets, weight, bias, cotangent):
    tile_rows, tile_cols, channels = (frames.shape[2], frames.shape[3], frames.shape[4])
    row_start = lax.axis_index("row") * tile_rows
    col_start = lax.axis_index("col") * tile_cols
    image_rows = lax.axis_size("row") * tile_rows
    image_cols = lax.axis_size("col") * tile_cols
    wide = MAXOFF + RAD + 1
    edge = (wide + 15) // 16 * 16
    side = 2 * RAD + 1
    width = (tile_cols + 2 * RAD + 15) // 16 * 16
    lanes = (side * width + 127) // 128 * 128
    window_rows = tile_rows + 2 * RAD
    pixels_one, pixels_two = tile_rows * tile_cols, window_rows * width
    long = max(pixels_two, (tile_rows - 1) * width + lanes)
    shift = offsets[0, row_start // BLK, col_start // BLK]
    place = jnp.concatenate([shift, jnp.stack([row_start, col_start])]).astype(jnp.int32)
    pad_one, pad_two = gather_halos(frames[0], wide, edge)
    whole = pl.BlockSpec(memory_space=pltpu.VMEM)
    rows = padded_rows(9 * channels + 1)
    geometry = (tile_rows, tile_cols, image_rows, image_cols, edge, width)
    corr, terms = pl.pallas_call(
        functools.partial(tile_kernel, geometry),
        out_shape=[
            jax.ShapeDtypeStruct((side * side, pixels_one), jnp.bfloat16),
            jax.ShapeDtypeStruct((2, rows, channels // 2), jnp.float32),
        ],
        in_specs=[pl.BlockSpec(memory_space=pltpu.SMEM)] + [whole] * 5,
        out_specs=[whole] * 2,
        scratch_shapes=[
            pltpu.VMEM(((tile_rows + 2) * tile_cols, 3 * channels), jnp.bfloat16),
            pltpu.VMEM(((window_rows + 2) * width, 3 * channels), jnp.bfloat16),
            pltpu.VMEM((pixels_one, channels), jnp.float32),
            pltpu.VMEM((pixels_two, channels), jnp.float32),
            pltpu.VMEM((pixels_one, channels), jnp.bfloat16),
            pltpu.VMEM((long, channels), jnp.bfloat16),
            pltpu.VMEM((pixels_one, channels), jnp.float32),
            pltpu.VMEM((channels, pixels_one), jnp.bfloat16),
            pltpu.VMEM((channels, pixels_two), jnp.bfloat16),
            pltpu.VMEM((long, channels), jnp.float32),
            pltpu.VMEM((side * side, pixels_one), jnp.float32),
            pltpu.VMEM((side * side, pixels_one), jnp.float32),
            pltpu.VMEM((lanes, 4 * tile_cols), jnp.float32),
        ],
        compiler_params=pltpu.CompilerParams(vmem_limit_bytes=48 * 2**20),
        name="tile_terms",
    )(
        place, pad_one, pad_two, weight.reshape(3, 3 * channels, channels), bias[None],
        cotangent[0].reshape(side * side, pixels_one),
    )
    summed = sum_everywhere(terms)
    grad_weight, grad_bias = pl.pallas_call(
        spread_kernel,
        out_shape=[
            jax.ShapeDtypeStruct((9 * channels, channels), jnp.float32),
            jax.ShapeDtypeStruct((1, channels), jnp.float32),
        ],
        in_specs=[whole],
        out_specs=[whole] * 2,
        compiler_params=pltpu.CompilerParams(vmem_limit_bytes=32 * 2**20),
        name="spread_sum",
    )(summed)
    return (
        corr.reshape(1, side * side, tile_rows, tile_cols),
        grad_weight.reshape(weight.shape),
        grad_bias[0],
    )


def solution(mesh):
    return jax.shard_map(
        shards,
        mesh=mesh,
        in_specs=(
            P("pair", None, "row", "col", None),
            P("pair", None, None, None),
            P(),
            P(),
            P("pair", None, "row", "col"),
        ),
        out_specs=(P("pair", None, "row", "col"), P(), P()),
        check_vma=False,
    )
```

```python
import functools

import jax
import jax.numpy as jnp
from jax import lax
from jax.experimental import pallas as pl
from jax.experimental.pallas import tpu as pltpu
from jax.sharding import PartitionSpec as P

BLK = 32
RAD = 4
MAXOFF = 8
MESH = pl.DeviceIdType.MESH


def exchange_plan():
    sizes = {axis: lax.axis_size(axis) for axis in ("row", "col")}
    bits = {
        axis: [1 << place for place in range(size.bit_length() - 1)]
        for axis, size in sizes.items()
    }
    near = [("row", stride) for stride in bits["row"][:1]]
    rest = [("row", stride) for stride in bits["row"][1:]]
    side = [("col", stride) for stride in reversed(bits["col"])]
    return [near + rest + side, near + side + rest]


def sum_kernel(plans, runs, terms, total, acc, send_half, recv_half, recv_wide, *sems):
    rs_send, rs_recv, ag_send, ag_recv, far_send, far_recv = sems
    count = len(plans[0])
    parts = range(len(runs))
    depth = lax.axis_size("pair")
    me = lax.axis_index("pair")

    def partner(step):
        axis, stride = step
        at = lax.axis_index(axis)
        bit = lax.rem(at // stride, 2)
        return bit, {axis: at + stride - 2 * stride * bit}

    def peer(hop):
        return lax.rem(me + hop, depth)

    barrier = pltpu.get_barrier_semaphore()
    for step in plans[0]:
        pl.semaphore_signal(barrier, inc=1, device_id=partner(step)[1], device_id_type=MESH)
    for hop in range(1, depth):
        pl.semaphore_signal(barrier, inc=1, device_id={"pair": peer(hop)}, device_id_type=MESH)
    pl.semaphore_wait(barrier, count + depth - 1)

    base = [start for _, start, _ in runs]
    trail = [[] for _ in parts]
    waiting = [None for _ in parts]
    sent = []

    def send(src, dst, send_sem, recv_sem, device):
        copy = pltpu.make_async_remote_copy(
            src_ref=src,
            dst_ref=dst,
            send_sem=send_sem,
            recv_sem=recv_sem,
            device_id=device,
            device_id_type=MESH,
        )
        copy.start()
        sent.append(copy)
        return copy

    def absorb(part, place):
        half, _, rows = runs[part]
        size = rows >> (place + 1)
        copy, keep, came = waiting[part]
        copy.wait_recv()
        source = terms if place == 0 else acc
        acc[half, pl.ds(keep, size), :] = source[half, pl.ds(keep, size), :] + came[...].astype(
            jnp.float32
        )
        base[part] = keep

    for place in range(count):
        for part in parts:
            half, start, rows = runs[part]
            size = rows >> (place + 1)
            slot = start + rows - (rows >> place)
            if place > 0:
                absorb(part, place - 1)
            bit, device = partner(plans[half][place])
            keep = pl.multiple_of(base[part] + bit * size, 16)
            give = pl.multiple_of(base[part] + (1 - bit) * size, 16)
            if place == 0:
                src = terms.at[half, pl.ds(give, size), :]
                dst = recv_wide.at[half, pl.ds(start // 2, size), :]
            else:
                send_half[half, slot : slot + size, :] = acc[half, pl.ds(give, size), :].astype(
                    jnp.bfloat16
                )
                src = send_half.at[half, pl.ds(slot, size), :]
                dst = recv_half.at[half, pl.ds(slot, size), :]
            copy = send(src, dst, rs_send.at[part, place], rs_recv.at[part, place], device)
            waiting[part] = (copy, keep, dst)
            trail[part].append(base[part])

    arrivals = [[] for _ in parts]
    for part in parts:
        half, start, rows = runs[part]
        absorb(part, count - 1)
        size = (rows >> count) // depth
        slot = start + rows - (rows >> count)
        for hop in range(1, depth):
            give = pl.multiple_of(base[part] + peer(hop) * size, 16)
            first = slot + (hop - 1) * size
            send_half[half, first : first + size, :] = acc[half, pl.ds(give, size), :].astype(
                jnp.bfloat16
            )
            src = send_half.at[half, pl.ds(first, size), :]
            dst = recv_half.at[half, pl.ds(first, size), :]
            copy = send(
                src, dst, far_send.at[part, hop], far_recv.at[part, hop], {"pair": peer(hop)}
            )
            arrivals[part].append((copy, dst))
    for part in parts:
        half, start, rows = runs[part]
        size = (rows >> count) // depth
        own = pl.ds(pl.multiple_of(base[part] + me * size, 16), size)
        value = acc[half, own, :]
        for copy, came in arrivals[part]:
            copy.wait_recv()
            value = value + came[...].astype(jnp.float32)
        total[half, own, :] = value.astype(jnp.bfloat16)
        block = total.at[half, own, :]
        arrivals[part] = [
            send(
                block,
                block,
                far_send.at[part, depth - 1 + hop],
                far_recv.at[part, depth - 1 + hop],
                {"pair": peer(hop)},
            )
            for hop in range(1, depth)
        ]
    for place in reversed(range(count)):
        for part in parts:
            half, start, rows = runs[part]
            size = rows >> (place + 1)
            for copy in arrivals[part]:
                copy.wait_recv()
            block = total.at[half, pl.ds(pl.multiple_of(base[part], 16), size), :]
            copy = send(
                block,
                block,
                ag_send.at[part, place],
                ag_recv.at[part, place],
                partner(plans[half][place])[1],
            )
            arrivals[part] = [copy]
            base[part] = trail[part][place]
    for part in parts:
        for copy in arrivals[part]:
            copy.wait_recv()
    for copy in sent:
        copy.wait_send()


def padded_rows(rows):
    devices = lax.axis_size("row") * lax.axis_size("col") * lax.axis_size("pair")
    grain = 16 * devices
    return (rows + grain - 1) // grain * grain


def sum_everywhere(terms):
    plans = exchange_plan()
    rows = terms.shape[1]
    grains = rows // padded_rows(1)
    head = (grains + 1) // 2 * padded_rows(1)
    runs = [(half, 0, head) for half in range(2)]
    if head < rows:
        runs += [(half, head, rows - head) for half in range(2)]
    near = pltpu.SemaphoreType.DMA((len(runs), len(plans[0])))
    far = pltpu.SemaphoreType.DMA((len(runs), 2 * lax.axis_size("pair")))
    return pl.pallas_call(
        functools.partial(sum_kernel, plans, runs),
        out_shape=jax.ShapeDtypeStruct(terms.shape, jnp.bfloat16),
        in_specs=[pl.BlockSpec(memory_space=pltpu.VMEM)],
        out_specs=pl.BlockSpec(memory_space=pltpu.VMEM),
        scratch_shapes=[
            pltpu.VMEM(terms.shape, jnp.float32),
            pltpu.VMEM(terms.shape, jnp.bfloat16),
            pltpu.VMEM(terms.shape, jnp.bfloat16),
            pltpu.VMEM(terms.shape, jnp.float32),
            near,
            near,
            near,
            near,
            far,
            far,
        ],
        compiler_params=pltpu.CompilerParams(
            collective_id=1, has_side_effects=True, vmem_limit_bytes=32 * 2**20
        ),
        name="sum_everywhere",
    )(terms)


def halo_kernel(
    wide, edge, frames, pad_one, pad_two, sides, cells, send_sem, recv_sem, own_sem
):
    row, col = lax.axis_index("row"), lax.axis_index("col")
    row_count, col_count = lax.axis_size("row"), lax.axis_size("col")
    tile_rows, tile_cols = frames.shape[1], frames.shape[2]
    ways = [(down, right) for down in (0, -1, 1) for right in (0, -1, 1) if (down, right) != (0, 0)]

    def lies(down, right):
        inside_rows = (row + down >= 0) & (row + down < row_count)
        inside_cols = (col + right >= 0) & (col + right < col_count)
        return inside_rows & inside_cols

    def device(down, right):
        return {"row": row + down, "col": col + right}

    def span(step, size, halo):
        if step == 0:
            return pl.ds(0, size), pl.ds(halo, size)
        if step > 0:
            return pl.ds(size - halo, halo), pl.ds(0, halo)
        return pl.ds(0, halo), pl.ds(halo + size, halo)

    barrier = pltpu.get_barrier_semaphore()
    for way in ways:
        @pl.when(lies(*way))
        def _():
            pl.semaphore_signal(barrier, inc=1, device_id=device(*way), device_id_type=MESH)
    first = frames[0, :, :edge, :].astype(jnp.float32)
    cells[0] = first[:, 0, :].astype(jnp.bfloat16)
    final = frames[0, :, tile_cols - edge :, :].astype(jnp.float32)
    cells[1] = final[:, edge - 1, :].astype(jnp.bfloat16)
    own = []
    for frame, (pad, halo) in enumerate(((pad_one, 1), (pad_two, wide))):
        middle = pad.at[pl.ds(halo, tile_rows), pl.ds(edge, tile_cols), :]
        own.append(pltpu.make_async_copy(frames.at[frame], middle, own_sem.at[frame]))
        own[-1].start()
    near_rows = 1 + (row > 0).astype(jnp.int32) + (row < row_count - 1).astype(jnp.int32)
    near_cols = 1 + (col > 0).astype(jnp.int32) + (col < col_count - 1).astype(jnp.int32)
    pl.semaphore_wait(barrier, near_rows * near_cols - 1)
    copies = []
    for place, way in enumerate(ways):
        for frame, (pad, halo) in enumerate(((pad_one, 1), (pad_two, wide))):
            take_rows, put_rows = span(way[0], tile_rows, halo)
            take_cols, put_cols = span(way[1], tile_cols, edge)
            source = frames.at[frame, take_rows, take_cols, :]
            target = pad.at[put_rows, put_cols, :]
            if frame == 0 and way[0] == 0:
                source = cells.at[1 if way[1] > 0 else 0]
                target = sides.at[0 if way[1] > 0 else 1]
            copy = pltpu.make_async_remote_copy(
                src_ref=source,
                dst_ref=target,
                send_sem=send_sem.at[place, frame],
                recv_sem=recv_sem.at[place, frame],
                device_id=device(*way),
                device_id_type=MESH,
            )
            copies.append((way, copy))
            pl.when(lies(*way))(copy.start)
    for copy in own:
        copy.wait()
    for way, copy in copies:
        pl.when(lies(-way[0], -way[1]))(copy.wait_recv)
    for way, copy in copies:
        pl.when(lies(*way))(copy.wait_send)


def gather_halos(frames, wide, edge):
    tile_rows, tile_cols, channels = frames.shape[1:]
    pads = [
        jax.ShapeDtypeStruct((tile_rows + 2 * halo, tile_cols + 2 * edge, channels), frames.dtype)
        for halo in (1, wide)
    ]
    pads.append(jax.ShapeDtypeStruct((2, tile_rows, channels), frames.dtype))
    whole = pl.BlockSpec(memory_space=pltpu.VMEM)
    return pl.pallas_call(
        functools.partial(halo_kernel, wide, edge),
        out_shape=pads,
        in_specs=[whole],
        out_specs=[whole] * 3,
        scratch_shapes=[
            pltpu.VMEM((2, tile_rows, channels), frames.dtype),
            pltpu.SemaphoreType.DMA((8, 2)),
            pltpu.SemaphoreType.DMA((8, 2)),
            pltpu.SemaphoreType.DMA((2,)),
        ],
        compiler_params=pltpu.CompilerParams(
            collective_id=0, has_side_effects=True, vmem_limit_bytes=16 * 2**20
        ),
        name="gather_halos",
    )(frames)


def tile_kernel(
    geometry, place, pad_one, pad_two, sides, weight, bias, cot, corr, terms,
    taps_one, taps_two, pre_one, pre_two, feat_one, feat_two, delta_one, flip_one, flip_two,
    grad_two, cot_wide, corr_wide, lanes_wide, sides_wide,
):
    tile_rows, tile_cols, image_rows, image_cols, edge, width = geometry
    channels = bias.shape[1]
    side = 2 * RAD + 1
    lanes = lanes_wide.shape[0]
    padded_cols = tile_cols + 2 * edge
    window_rows = tile_rows + 2 * RAD
    pixels_two = window_rows * width
    shift_row, shift_col, row_start, col_start = place[0], place[1], place[2], place[3]
    inv_root = channels ** (-0.5)

    across = lax.broadcasted_iota(jnp.int32, (padded_cols, channels), 0) + (col_start - edge)
    inside_cols = (across >= 0) & (across < image_cols)

    def masked(line, image_row):
        inside = inside_cols & (image_row >= 0) & (image_row < image_rows)
        return jnp.where(inside, line.astype(jnp.float32), 0.0)

    sides_wide[:, :8, :] = jnp.zeros_like(sides_wide[:, :8, :])
    sides_wide[:, 8 : 8 + tile_rows, :] = sides[...].astype(jnp.float32)
    sides_wide[:, 8 + tile_rows :, :] = jnp.zeros_like(sides_wide[:, 8 + tile_rows :, :])
    spot = across - (col_start - edge)

    @pl.loop(0, tile_rows + 2)
    def _(line):
        cells = pad_one[line].astype(jnp.float32)
        middle = (line > 0) & (line < tile_rows + 1)
        for end, column in enumerate((edge - 1, edge + tile_cols)):
            side_line = sides_wide[end, pl.ds(line + 7, 1), :]
            cells = jnp.where((spot == column) & middle, side_line, cells)
        cells = masked(cells, row_start - 1 + line)
        for tap in range(3):
            first = edge - 1 + tap
            taps_one[pl.ds(pl.multiple_of(line * tile_cols, 16), tile_cols),
                     tap * channels : (tap + 1) * channels] = (
                cells[first : first + tile_cols].astype(jnp.bfloat16)
            )

    @pl.loop(0, window_rows + 2)
    def _(line):
        at = shift_row + MAXOFF + line
        cells = masked(pad_two[at], row_start - (MAXOFF + RAD + 1) + at)
        cells = pltpu.roll(cells, padded_cols - (shift_col + edge - RAD - 1), 0)
        for tap in range(3):
            taps_two[pl.ds(pl.multiple_of(line * width, 16), width),
                     tap * channels : (tap + 1) * channels] = (
                cells[tap : tap + width].astype(jnp.bfloat16)
            )

    def convolved(taps, first, size, pitch):
        total = jnp.broadcast_to(bias[...], (size, channels))
        for tap in range(3):
            total = total + jnp.dot(
                taps[pl.ds(pl.multiple_of(first + tap * pitch, 16), size), :],
                weight[tap],
                preferred_element_type=jnp.float32,
            )
        return total

    group = 4
    size_one = group * tile_cols

    @pl.loop(0, tile_rows // group)
    def _(block):
        first = pl.multiple_of(block * size_one, 16)
        pre = convolved(taps_one, first, size_one, tile_cols)
        pre_one[pl.ds(first, size_one), :] = pre
        feat_one[pl.ds(first, size_one), :] = jnp.maximum(pre, 0.0).astype(jnp.bfloat16)

    size_two = group * width

    @pl.loop(0, window_rows // group)
    def _(block):
        first = pl.multiple_of(block * size_two, 16)
        pre = convolved(taps_two, first, size_two, width).reshape(group, width, channels)
        rows = lax.broadcasted_iota(jnp.int32, pre.shape, 0) + (
            row_start + shift_row - RAD + block * group
        )
        cols = lax.broadcasted_iota(jnp.int32, pre.shape, 1) + (col_start + shift_col - RAD)
        inside = (rows >= 0) & (rows < image_rows) & (cols >= 0) & (cols < image_cols)
        pre = jnp.where(inside, pre, 0.0).reshape(size_two, channels)
        pre_two[pl.ds(first, size_two), :] = pre
        feat_two[pl.ds(first, size_two), :] = jnp.maximum(pre, 0.0).astype(jnp.bfloat16)

    feat_two[pixels_two:, :] = jnp.zeros_like(feat_two[pixels_two:, :])
    grad_two[...] = jnp.zeros_like(grad_two)
    cot_wide[...] = cot[...].astype(jnp.float32)
    lanes_wide[...] = jnp.zeros_like(lanes_wide)

    def skew(cells, back):
        line = lax.rem(lax.broadcasted_iota(jnp.int32, cells.shape, 0), tile_cols)
        step = 1
        while step < tile_cols:
            moved = pltpu.roll(cells, lanes - step if back else step, 1)
            cells = jnp.where((line // step) % 2 == 1, moved, cells)
            step *= 2
        return cells

    @pl.loop(0, tile_rows // group)
    def _(block):
        at = pl.ds(pl.multiple_of(block * size_one, 128), size_one)
        for line in range(side):
            lanes_wide[line * width : line * width + side, :] = cot_wide[
                line * side : (line + 1) * side, at
            ]
        spread_all = skew(lanes_wide[...].T, False).astype(jnp.bfloat16)
        score_list = []
        for inner in range(group):
            row = block * group + inner
            spread = spread_all[inner * tile_cols : (inner + 1) * tile_cols]
            pixels = pl.ds(pl.multiple_of(row * tile_cols, 16), tile_cols)
            window = pl.ds(pl.multiple_of(row * width, 16), lanes)
            one, two = feat_one[pixels, :], feat_two[window, :]
            score_list.append(
                lax.dot_general(one, two, (((1,), (1,)), ((), ())), preferred_element_type=jnp.float32)
            )
            grad = jnp.dot(spread, two, preferred_element_type=jnp.float32) * inv_root
            grad = jnp.where(pre_one[pixels, :] > 0, grad, 0.0)
            delta_one[pixels, :] = grad.astype(jnp.bfloat16).astype(jnp.float32)
            grad_two[window, :] += lax.dot_general(
                spread, one, (((0,), (0,)), ((), ())), preferred_element_type=jnp.float32
            )
        scores = skew(jnp.concatenate(score_list, axis=0), True).T * inv_root
        for line in range(side):
            corr_wide[line * side : (line + 1) * side, at] = scores[
                line * width : line * width + side
            ]

    corr[...] = corr_wide[...].astype(jnp.bfloat16)
    delta_two = jnp.where(pre_two[...] > 0, grad_two[:pixels_two, :] * inv_root, 0.0)
    bias_term = jnp.sum(delta_one[...], axis=0, keepdims=True)
    bias_term = bias_term + jnp.sum(delta_two, axis=0, keepdims=True)
    flip_one[...] = delta_one[...].T.astype(jnp.bfloat16)
    flip_two[...] = delta_two.T.astype(jnp.bfloat16)

    half = channels // 2
    pixels_one = tile_rows * tile_cols
    for tap_row in range(3):
        for tap_col in range(3):
            cols = slice(tap_col * channels, (tap_col + 1) * channels)
            first_one, first_two = tap_row * tile_cols, tap_row * width
            term = jnp.dot(
                flip_one[...],
                taps_one[first_one : first_one + pixels_one, cols],
                preferred_element_type=jnp.float32,
            ) + jnp.dot(
                flip_two[...],
                taps_two[first_two : first_two + pixels_two, cols],
                preferred_element_type=jnp.float32,
            )
            term = term.T
            first = (tap_row * 3 + tap_col) * channels
            terms[0, first : first + channels, :] = term[:, :half]
            terms[1, first : first + channels, :] = term[:, half:]
    last = 9 * channels
    rest = terms.shape[1] - last
    filler = lax.broadcasted_iota(jnp.int32, (rest, channels), 0) == 0
    filler = jnp.where(filler, jnp.broadcast_to(bias_term, (rest, channels)), 0.0)
    terms[0, last:, :] = filler[:, :half]
    terms[1, last:, :] = filler[:, half:]


def spread_kernel(summed, grad_weight, grad_bias):
    rows, half = grad_weight.shape[0], summed.shape[2]
    for part in range(2):
        lanes = slice(part * half, (part + 1) * half)
        grad_weight[:, lanes] = summed[part, :rows, :].astype(jnp.float32)
        grad_bias[:, lanes] = summed[part, rows : rows + 16, :].astype(jnp.float32)[:1]


def shards(frames, offsets, weight, bias, cotangent):
    tile_rows, tile_cols, channels = (frames.shape[2], frames.shape[3], frames.shape[4])
    row_start = lax.axis_index("row") * tile_rows
    col_start = lax.axis_index("col") * tile_cols
    image_rows = lax.axis_size("row") * tile_rows
    image_cols = lax.axis_size("col") * tile_cols
    wide = MAXOFF + RAD + 1
    edge = (wide + 15) // 16 * 16
    side = 2 * RAD + 1
    width = (tile_cols + 2 * RAD + 15) // 16 * 16
    lanes = (side * width + 127) // 128 * 128
    window_rows = tile_rows + 2 * RAD
    pixels_one, pixels_two = tile_rows * tile_cols, window_rows * width
    long = max(pixels_two, (tile_rows - 1) * width + lanes)
    shift = offsets[0, row_start // BLK, col_start // BLK]
    place = jnp.concatenate([shift, jnp.stack([row_start, col_start])]).astype(jnp.int32)
    pad_one, pad_two, sides = gather_halos(frames[0], wide, edge)
    whole = pl.BlockSpec(memory_space=pltpu.VMEM)
    rows = padded_rows(9 * channels + 1)
    geometry = (tile_rows, tile_cols, image_rows, image_cols, edge, width)
    corr, terms = pl.pallas_call(
        functools.partial(tile_kernel, geometry),
        out_shape=[
            jax.ShapeDtypeStruct((side * side, pixels_one), jnp.bfloat16),
            jax.ShapeDtypeStruct((2, rows, channels // 2), jnp.float32),
        ],
        in_specs=[pl.BlockSpec(memory_space=pltpu.SMEM)] + [whole] * 6,
        out_specs=[whole] * 2,
        scratch_shapes=[
            pltpu.VMEM(((tile_rows + 2) * tile_cols, 3 * channels), jnp.bfloat16),
            pltpu.VMEM(((window_rows + 2) * width, 3 * channels), jnp.bfloat16),
            pltpu.VMEM((pixels_one, channels), jnp.float32),
            pltpu.VMEM((pixels_two, channels), jnp.float32),
            pltpu.VMEM((pixels_one, channels), jnp.bfloat16),
            pltpu.VMEM((long, channels), jnp.bfloat16),
            pltpu.VMEM((pixels_one, channels), jnp.float32),
            pltpu.VMEM((channels, pixels_one), jnp.bfloat16),
            pltpu.VMEM((channels, pixels_two), jnp.bfloat16),
            pltpu.VMEM((long, channels), jnp.float32),
            pltpu.VMEM((side * side, pixels_one), jnp.float32),
            pltpu.VMEM((side * side, pixels_one), jnp.float32),
            pltpu.VMEM((lanes, 4 * tile_cols), jnp.float32),
            pltpu.VMEM((2, tile_rows + 16, channels), jnp.float32),
        ],
        compiler_params=pltpu.CompilerParams(vmem_limit_bytes=48 * 2**20),
        name="tile_terms",
    )(
        place, pad_one, pad_two, sides, weight.reshape(3, 3 * channels, channels), bias[None],
        cotangent[0].reshape(side * side, pixels_one),
    )
    summed = sum_everywhere(terms)
    grad_weight, grad_bias = pl.pallas_call(
        spread_kernel,
        out_shape=[
            jax.ShapeDtypeStruct((9 * channels, channels), jnp.float32),
            jax.ShapeDtypeStruct((1, channels), jnp.float32),
        ],
        in_specs=[whole],
        out_specs=[whole] * 2,
        compiler_params=pltpu.CompilerParams(vmem_limit_bytes=32 * 2**20),
        name="spread_sum",
    )(summed)
    return (
        corr.reshape(1, side * side, tile_rows, tile_cols),
        grad_weight.reshape(weight.shape),
        grad_bias[0],
    )


def solution(mesh):
    return jax.shard_map(
        shards,
        mesh=mesh,
        in_specs=(
            P("pair", None, "row", "col", None),
            P("pair", None, None, None),
            P(),
            P(),
            P("pair", None, "row", "col"),
        ),
        out_specs=(P("pair", None, "row", "col"), P(), P()),
        check_vma=False,
    )
```

```python
import functools

import jax
import jax.numpy as jnp
from jax import lax
from jax.experimental import pallas as pl
from jax.experimental.pallas import tpu as pltpu
from jax.sharding import PartitionSpec as P

BLK = 32
RAD = 4
MAXOFF = 8
MESH = pl.DeviceIdType.MESH


def skew(cells, period, back):
    lanes = cells.shape[1]
    line = lax.rem(lax.broadcasted_iota(jnp.int32, cells.shape, 0), period)
    step = 1
    while step < period:
        moved = pltpu.roll(cells, lanes - step if back else step, 1)
        cells = jnp.where((line // step) % 2 == 1, moved, cells)
        step *= 2
    return cells


def exchange_plan():
    sizes = {axis: lax.axis_size(axis) for axis in ("row", "col")}
    bits = {
        axis: [1 << place for place in range(size.bit_length() - 1)]
        for axis, size in sizes.items()
    }
    near = [("row", stride) for stride in bits["row"][:1]]
    rest = [("row", stride) for stride in bits["row"][1:]]
    side = [("col", stride) for stride in reversed(bits["col"])]
    return [near + rest + side, near + side + rest]


def sum_kernel(
    plans, runs, shape, terms, scores, total, corr,
    acc, send_half, recv_half, recv_wide, corr_wide, *sems,
):
    rs_send, rs_recv, ag_send, ag_recv, far_send, far_recv = sems
    count = len(plans[0])
    parts = range(len(runs))
    depth = lax.axis_size("pair")
    me = lax.axis_index("pair")

    def partner(step):
        axis, stride = step
        at = lax.axis_index(axis)
        bit = lax.rem(at // stride, 2)
        return bit, {axis: at + stride - 2 * stride * bit}

    def peer(hop):
        return lax.rem(me + hop, depth)

    barrier = pltpu.get_barrier_semaphore()
    for step in plans[0]:
        pl.semaphore_signal(barrier, inc=1, device_id=partner(step)[1], device_id_type=MESH)
    for hop in range(1, depth):
        pl.semaphore_signal(barrier, inc=1, device_id={"pair": peer(hop)}, device_id_type=MESH)
    pl.semaphore_wait(barrier, count + depth - 1)

    tile_cols, width, group, inv_root = shape
    side = 2 * RAD + 1
    chunk = group * tile_cols
    blocks = list(range(scores.shape[0] // chunk))

    def take_band():
        if not blocks:
            return
        at = slice(blocks[0] * chunk, (blocks[0] + 1) * chunk)
        bands = skew(scores[at, :], tile_cols, True).T * inv_root
        for line in range(side):
            corr_wide[line * side : (line + 1) * side, at] = bands[
                line * width : line * width + side
            ]
        blocks.pop(0)
        if not blocks:
            corr[...] = corr_wide[...].astype(jnp.bfloat16)

    base = [start for _, start, _ in runs]
    trail = [[] for _ in parts]
    waiting = [None for _ in parts]
    sent = []

    def send(src, dst, send_sem, recv_sem, device):
        copy = pltpu.make_async_remote_copy(
            src_ref=src,
            dst_ref=dst,
            send_sem=send_sem,
            recv_sem=recv_sem,
            device_id=device,
            device_id_type=MESH,
        )
        copy.start()
        sent.append(copy)
        return copy

    def absorb(part, place):
        half, _, rows = runs[part]
        size = rows >> (place + 1)
        copy, keep, came = waiting[part]
        copy.wait_recv()
        source = terms if place == 0 else acc
        acc[half, pl.ds(keep, size), :] = source[half, pl.ds(keep, size), :] + came[...].astype(
            jnp.float32
        )
        base[part] = keep

    for place in range(count):
        for part in parts:
            half, start, rows = runs[part]
            size = rows >> (place + 1)
            slot = start + rows - (rows >> place)
            if place > 0:
                absorb(part, place - 1)
            bit, device = partner(plans[half][place])
            keep = pl.multiple_of(base[part] + bit * size, 16)
            give = pl.multiple_of(base[part] + (1 - bit) * size, 16)
            if place == 0:
                src = terms.at[half, pl.ds(give, size), :]
                dst = recv_wide.at[half, pl.ds(start // 2, size), :]
            else:
                send_half[half, slot : slot + size, :] = acc[half, pl.ds(give, size), :].astype(
                    jnp.bfloat16
                )
                src = send_half.at[half, pl.ds(slot, size), :]
                dst = recv_half.at[half, pl.ds(slot, size), :]
            copy = send(src, dst, rs_send.at[part, place], rs_recv.at[part, place], device)
            waiting[part] = (copy, keep, dst)
            trail[part].append(base[part])
        take_band()

    arrivals = [[] for _ in parts]
    for part in parts:
        half, start, rows = runs[part]
        absorb(part, count - 1)
        size = (rows >> count) // depth
        slot = start + rows - (rows >> count)
        for hop in range(1, depth):
            give = pl.multiple_of(base[part] + peer(hop) * size, 16)
            first = slot + (hop - 1) * size
            send_half[half, first : first + size, :] = acc[half, pl.ds(give, size), :].astype(
                jnp.bfloat16
            )
            src = send_half.at[half, pl.ds(first, size), :]
            dst = recv_half.at[half, pl.ds(first, size), :]
            copy = send(
                src, dst, far_send.at[part, hop], far_recv.at[part, hop], {"pair": peer(hop)}
            )
            arrivals[part].append((copy, dst))
    take_band()
    for part in parts:
        half, start, rows = runs[part]
        size = (rows >> count) // depth
        own = pl.ds(pl.multiple_of(base[part] + me * size, 16), size)
        value = acc[half, own, :]
        for copy, came in arrivals[part]:
            copy.wait_recv()
            value = value + came[...].astype(jnp.float32)
        total[half, own, :] = value.astype(jnp.bfloat16)
        block = total.at[half, own, :]
        arrivals[part] = [
            send(
                block,
                block,
                far_send.at[part, depth - 1 + hop],
                far_recv.at[part, depth - 1 + hop],
                {"pair": peer(hop)},
            )
            for hop in range(1, depth)
        ]
    for place in reversed(range(count)):
        for part in parts:
            half, start, rows = runs[part]
            size = rows >> (place + 1)
            for copy in arrivals[part]:
                copy.wait_recv()
            block = total.at[half, pl.ds(pl.multiple_of(base[part], 16), size), :]
            copy = send(
                block,
                block,
                ag_send.at[part, place],
                ag_recv.at[part, place],
                partner(plans[half][place])[1],
            )
            arrivals[part] = [copy]
            base[part] = trail[part][place]
        take_band()
    while blocks:
        take_band()
    for part in parts:
        for copy in arrivals[part]:
            copy.wait_recv()
    for copy in sent:
        copy.wait_send()


def padded_rows(rows):
    devices = lax.axis_size("row") * lax.axis_size("col") * lax.axis_size("pair")
    grain = 16 * devices
    return (rows + grain - 1) // grain * grain


def sum_everywhere(terms, scores, shape):
    plans = exchange_plan()
    rows = terms.shape[1]
    grains = rows // padded_rows(1)
    head = (grains + 1) // 2 * padded_rows(1)
    runs = [(half, 0, head) for half in range(2)]
    if head < rows:
        runs += [(half, head, rows - head) for half in range(2)]
    near = pltpu.SemaphoreType.DMA((len(runs), len(plans[0])))
    far = pltpu.SemaphoreType.DMA((len(runs), 2 * lax.axis_size("pair")))
    return pl.pallas_call(
        functools.partial(sum_kernel, plans, runs, shape),
        out_shape=[
            jax.ShapeDtypeStruct(terms.shape, jnp.bfloat16),
            jax.ShapeDtypeStruct(((2 * RAD + 1) ** 2, scores.shape[0]), jnp.bfloat16),
        ],
        in_specs=[pl.BlockSpec(memory_space=pltpu.VMEM)] * 2,
        out_specs=[pl.BlockSpec(memory_space=pltpu.VMEM)] * 2,
        scratch_shapes=[
            pltpu.VMEM(terms.shape, jnp.float32),
            pltpu.VMEM(terms.shape, jnp.bfloat16),
            pltpu.VMEM(terms.shape, jnp.bfloat16),
            pltpu.VMEM(terms.shape, jnp.float32),
            pltpu.VMEM(((2 * RAD + 1) ** 2, scores.shape[0]), jnp.float32),
            near,
            near,
            near,
            near,
            far,
            far,
        ],
        compiler_params=pltpu.CompilerParams(
            collective_id=1, has_side_effects=True, vmem_limit_bytes=32 * 2**20
        ),
        name="sum_everywhere",
    )(terms, scores)


def halo_kernel(
    wide, edge, width, group, frames, cot, pad_one, pad_two, sides, spread,
    cells, cot_wide, lanes_wide, send_sem, recv_sem, own_sem,
):
    row, col = lax.axis_index("row"), lax.axis_index("col")
    row_count, col_count = lax.axis_size("row"), lax.axis_size("col")
    tile_rows, tile_cols = frames.shape[1], frames.shape[2]
    ways = [(down, right) for down in (0, -1, 1) for right in (0, -1, 1) if (down, right) != (0, 0)]

    def lies(down, right):
        inside_rows = (row + down >= 0) & (row + down < row_count)
        inside_cols = (col + right >= 0) & (col + right < col_count)
        return inside_rows & inside_cols

    def device(down, right):
        return {"row": row + down, "col": col + right}

    def span(step, size, halo):
        if step == 0:
            return pl.ds(0, size), pl.ds(halo, size)
        if step > 0:
            return pl.ds(size - halo, halo), pl.ds(0, halo)
        return pl.ds(0, halo), pl.ds(halo + size, halo)

    barrier = pltpu.get_barrier_semaphore()
    for way in ways:
        @pl.when(lies(*way))
        def _():
            pl.semaphore_signal(barrier, inc=1, device_id=device(*way), device_id_type=MESH)
    first = frames[0, :, :edge, :].astype(jnp.float32)
    cells[0] = first[:, 0, :].astype(jnp.bfloat16)
    final = frames[0, :, tile_cols - edge :, :].astype(jnp.float32)
    cells[1] = final[:, edge - 1, :].astype(jnp.bfloat16)
    own = []
    for frame, (pad, halo) in enumerate(((pad_one, 1), (pad_two, wide))):
        middle = pad.at[pl.ds(halo, tile_rows), pl.ds(edge, tile_cols), :]
        own.append(pltpu.make_async_copy(frames.at[frame], middle, own_sem.at[frame]))
        own[-1].start()
    near_rows = 1 + (row > 0).astype(jnp.int32) + (row < row_count - 1).astype(jnp.int32)
    near_cols = 1 + (col > 0).astype(jnp.int32) + (col < col_count - 1).astype(jnp.int32)
    pl.semaphore_wait(barrier, near_rows * near_cols - 1)
    copies = []
    for place, way in enumerate(ways):
        for frame, (pad, halo) in enumerate(((pad_one, 1), (pad_two, wide))):
            take_rows, put_rows = span(way[0], tile_rows, halo)
            take_cols, put_cols = span(way[1], tile_cols, edge)
            source = frames.at[frame, take_rows, take_cols, :]
            target = pad.at[put_rows, put_cols, :]
            if frame == 0 and way[0] == 0:
                source = cells.at[1 if way[1] > 0 else 0]
                target = sides.at[0 if way[1] > 0 else 1]
            copy = pltpu.make_async_remote_copy(
                src_ref=source,
                dst_ref=target,
                send_sem=send_sem.at[place, frame],
                recv_sem=recv_sem.at[place, frame],
                device_id=device(*way),
                device_id_type=MESH,
            )
            copies.append((way, copy))
            pl.when(lies(*way))(copy.start)
    side = 2 * RAD + 1
    chunk = group * tile_cols
    cot_wide[...] = cot[...].astype(jnp.float32)
    lanes_wide[...] = jnp.zeros_like(lanes_wide)
    for block in range(spread.shape[0] // chunk):
        at = slice(block * chunk, (block + 1) * chunk)
        for line in range(side):
            lanes_wide[line * width : line * width + side, :] = cot_wide[
                line * side : (line + 1) * side, at
            ]
        spread[at, :] = skew(lanes_wide[...].T, tile_cols, False).astype(jnp.bfloat16)
    for copy in own:
        copy.wait()
    for way, copy in copies:
        pl.when(lies(-way[0], -way[1]))(copy.wait_recv)
    for way, copy in copies:
        pl.when(lies(*way))(copy.wait_send)


def gather_halos(frames, cot, wide, edge, width, group, lanes):
    tile_rows, tile_cols, channels = frames.shape[1:]
    pads = [
        jax.ShapeDtypeStruct((tile_rows + 2 * halo, tile_cols + 2 * edge, channels), frames.dtype)
        for halo in (1, wide)
    ]
    pads.append(jax.ShapeDtypeStruct((2, tile_rows, channels), frames.dtype))
    pads.append(jax.ShapeDtypeStruct((cot.shape[1], lanes), cot.dtype))
    whole = pl.BlockSpec(memory_space=pltpu.VMEM)
    return pl.pallas_call(
        functools.partial(halo_kernel, wide, edge, width, group),
        out_shape=pads,
        in_specs=[whole] * 2,
        out_specs=[whole] * 4,
        scratch_shapes=[
            pltpu.VMEM((2, tile_rows, channels), frames.dtype),
            pltpu.VMEM(cot.shape, jnp.float32),
            pltpu.VMEM((lanes, group * tile_cols), jnp.float32),
            pltpu.SemaphoreType.DMA((8, 2)),
            pltpu.SemaphoreType.DMA((8, 2)),
            pltpu.SemaphoreType.DMA((2,)),
        ],
        compiler_params=pltpu.CompilerParams(
            collective_id=0, has_side_effects=True, vmem_limit_bytes=16 * 2**20
        ),
        name="gather_halos",
    )(frames, cot)


def tile_kernel(
    geometry, place, pad_one, pad_two, sides, spread_all, weight_far, bias, scores, terms,
    taps_one, taps_two, pre_one, pre_two, feat_one, feat_two, delta_one, flip_one, flip_two,
    grad_two, sides_wide, weight, weight_sem,
):
    tile_rows, tile_cols, image_rows, image_cols, edge, width, group = geometry
    channels = bias.shape[1]
    load = pltpu.make_async_copy(weight_far, weight, weight_sem)
    load.start()
    lanes = spread_all.shape[1]
    padded_cols = tile_cols + 2 * edge
    window_rows = tile_rows + 2 * RAD
    pixels_two = window_rows * width
    shift_row, shift_col, row_start, col_start = place[0], place[1], place[2], place[3]
    inv_root = channels ** (-0.5)

    across = lax.broadcasted_iota(jnp.int32, (padded_cols, channels), 0) + (col_start - edge)
    inside_cols = (across >= 0) & (across < image_cols)

    def masked(line, image_row):
        inside = inside_cols & (image_row >= 0) & (image_row < image_rows)
        return jnp.where(inside, line.astype(jnp.float32), 0.0)

    sides_wide[:, :8, :] = jnp.zeros_like(sides_wide[:, :8, :])
    sides_wide[:, 8 : 8 + tile_rows, :] = sides[...].astype(jnp.float32)
    sides_wide[:, 8 + tile_rows :, :] = jnp.zeros_like(sides_wide[:, 8 + tile_rows :, :])
    spot = across - (col_start - edge)

    @pl.loop(0, tile_rows + 2, unroll=2)
    def _(line):
        cells = pad_one[line].astype(jnp.float32)
        middle = (line > 0) & (line < tile_rows + 1)
        for end, column in enumerate((edge - 1, edge + tile_cols)):
            side_line = sides_wide[end, pl.ds(line + 7, 1), :]
            cells = jnp.where((spot == column) & middle, side_line, cells)
        cells = masked(cells, row_start - 1 + line)
        for tap in range(3):
            first = edge - 1 + tap
            taps_one[pl.ds(pl.multiple_of(line * tile_cols, 16), tile_cols),
                     tap * channels : (tap + 1) * channels] = (
                cells[first : first + tile_cols].astype(jnp.bfloat16)
            )

    @pl.loop(0, window_rows + 2, unroll=2)
    def _(line):
        at = shift_row + MAXOFF + line
        cells = masked(pad_two[at], row_start - (MAXOFF + RAD + 1) + at)
        cells = pltpu.roll(cells, padded_cols - (shift_col + edge - RAD - 1), 0)
        for tap in range(3):
            taps_two[pl.ds(pl.multiple_of(line * width, 16), width),
                     tap * channels : (tap + 1) * channels] = (
                cells[tap : tap + width].astype(jnp.bfloat16)
            )

    def convolved(taps, first, size, pitch):
        total = jnp.broadcast_to(bias[...], (size, channels))
        for tap in range(3):
            total = total + jnp.dot(
                taps[pl.ds(pl.multiple_of(first + tap * pitch, 16), size), :],
                weight[tap],
                preferred_element_type=jnp.float32,
            )
        return total

    load.wait()
    size_one = group * tile_cols

    @pl.loop(0, tile_rows // group)
    def _(block):
        first = pl.multiple_of(block * size_one, 16)
        pre = convolved(taps_one, first, size_one, tile_cols)
        pre_one[pl.ds(first, size_one), :] = pre
        feat_one[pl.ds(first, size_one), :] = jnp.maximum(pre, 0.0).astype(jnp.bfloat16)

    size_two = group * width

    @pl.loop(0, window_rows // group, unroll=2)
    def _(block):
        first = pl.multiple_of(block * size_two, 16)
        pre = convolved(taps_two, first, size_two, width).reshape(group, width, channels)
        rows = lax.broadcasted_iota(jnp.int32, pre.shape, 0) + (
            row_start + shift_row - RAD + block * group
        )
        cols = lax.broadcasted_iota(jnp.int32, pre.shape, 1) + (col_start + shift_col - RAD)
        inside = (rows >= 0) & (rows < image_rows) & (cols >= 0) & (cols < image_cols)
        pre = jnp.where(inside, pre, 0.0).reshape(size_two, channels)
        pre_two[pl.ds(first, size_two), :] = pre
        feat_two[pl.ds(first, size_two), :] = jnp.maximum(pre, 0.0).astype(jnp.bfloat16)

    feat_two[pixels_two:, :] = jnp.zeros_like(feat_two[pixels_two:, :])
    grad_two[...] = jnp.zeros_like(grad_two)

    @pl.loop(0, tile_rows // group)
    def _(block):
        for inner in range(group):
            row = block * group + inner
            pixels = pl.ds(pl.multiple_of(row * tile_cols, 16), tile_cols)
            window = pl.ds(pl.multiple_of(row * width, 16), lanes)
            spread = spread_all[pixels, :]
            one, two = feat_one[pixels, :], feat_two[window, :]
            scores[pixels, :] = lax.dot_general(
                one, two, (((1,), (1,)), ((), ())), preferred_element_type=jnp.float32
            )
            grad = jnp.dot(spread, two, preferred_element_type=jnp.float32) * inv_root
            grad = jnp.where(pre_one[pixels, :] > 0, grad, 0.0)
            delta_one[pixels, :] = grad.astype(jnp.bfloat16).astype(jnp.float32)
            grad_two[window, :] += lax.dot_general(
                spread, one, (((0,), (0,)), ((), ())), preferred_element_type=jnp.float32
            )

    delta_two = jnp.where(pre_two[...] > 0, grad_two[:pixels_two, :] * inv_root, 0.0)
    bias_term = jnp.sum(delta_one[...], axis=0, keepdims=True)
    bias_term = bias_term + jnp.sum(delta_two, axis=0, keepdims=True)
    flip_one[...] = delta_one[...].T.astype(jnp.bfloat16)
    flip_two[...] = delta_two.T.astype(jnp.bfloat16)

    half = channels // 2
    pixels_one = tile_rows * tile_cols
    for tap_row in range(3):
        for tap_col in range(3):
            cols = slice(tap_col * channels, (tap_col + 1) * channels)
            first_one, first_two = tap_row * tile_cols, tap_row * width
            term = jnp.dot(
                flip_one[...],
                taps_one[first_one : first_one + pixels_one, cols],
                preferred_element_type=jnp.float32,
            ) + jnp.dot(
                flip_two[...],
                taps_two[first_two : first_two + pixels_two, cols],
                preferred_element_type=jnp.float32,
            )
            term = term.T
            first = (tap_row * 3 + tap_col) * channels
            terms[0, first : first + channels, :] = term[:, :half]
            terms[1, first : first + channels, :] = term[:, half:]
    last = 9 * channels
    rest = terms.shape[1] - last
    filler = lax.broadcasted_iota(jnp.int32, (rest, channels), 0) == 0
    filler = jnp.where(filler, jnp.broadcast_to(bias_term, (rest, channels)), 0.0)
    terms[0, last:, :] = filler[:, :half]
    terms[1, last:, :] = filler[:, half:]


def spread_kernel(summed, grad_weight, grad_bias):
    rows, half = grad_weight.shape[0], summed.shape[2]
    for part in range(2):
        lanes = slice(part * half, (part + 1) * half)
        grad_weight[:, lanes] = summed[part, :rows, :].astype(jnp.float32)
        grad_bias[:, lanes] = summed[part, rows : rows + 16, :].astype(jnp.float32)[:1]


def shards(frames, offsets, weight, bias, cotangent):
    tile_rows, tile_cols, channels = (frames.shape[2], frames.shape[3], frames.shape[4])
    row_start = lax.axis_index("row") * tile_rows
    col_start = lax.axis_index("col") * tile_cols
    image_rows = lax.axis_size("row") * tile_rows
    image_cols = lax.axis_size("col") * tile_cols
    wide = MAXOFF + RAD + 1
    edge = (wide + 15) // 16 * 16
    side = 2 * RAD + 1
    width = (tile_cols + 2 * RAD + 15) // 16 * 16
    lanes = (side * width + 127) // 128 * 128
    window_rows = tile_rows + 2 * RAD
    pixels_one, pixels_two = tile_rows * tile_cols, window_rows * width
    long = max(pixels_two, (tile_rows - 1) * width + lanes)
    shift = offsets[0, row_start // BLK, col_start // BLK]
    place = jnp.concatenate([shift, jnp.stack([row_start, col_start])]).astype(jnp.int32)
    group = 4
    cot = cotangent[0].reshape(side * side, pixels_one)
    pad_one, pad_two, sides, spread = gather_halos(
        frames[0], cot, wide, edge, width, group, lanes
    )
    whole = pl.BlockSpec(memory_space=pltpu.VMEM)
    rows = padded_rows(9 * channels + 1)
    geometry = (tile_rows, tile_cols, image_rows, image_cols, edge, width, group)
    scores, terms = pl.pallas_call(
        functools.partial(tile_kernel, geometry),
        out_shape=[
            jax.ShapeDtypeStruct((pixels_one, lanes), jnp.float32),
            jax.ShapeDtypeStruct((2, rows, channels // 2), jnp.float32),
        ],
        in_specs=[pl.BlockSpec(memory_space=pltpu.SMEM)]
        + [whole] * 4
        + [pl.BlockSpec(memory_space=pl.ANY), whole],
        out_specs=[whole] * 2,
        scratch_shapes=[
            pltpu.VMEM(((tile_rows + 2) * tile_cols, 3 * channels), jnp.bfloat16),
            pltpu.VMEM(((window_rows + 2) * width, 3 * channels), jnp.bfloat16),
            pltpu.VMEM((pixels_one, channels), jnp.float32),
            pltpu.VMEM((pixels_two, channels), jnp.float32),
            pltpu.VMEM((pixels_one, channels), jnp.bfloat16),
            pltpu.VMEM((long, channels), jnp.bfloat16),
            pltpu.VMEM((pixels_one, channels), jnp.float32),
            pltpu.VMEM((channels, pixels_one), jnp.bfloat16),
            pltpu.VMEM((channels, pixels_two), jnp.bfloat16),
            pltpu.VMEM((long, channels), jnp.float32),
            pltpu.VMEM((2, tile_rows + 16, channels), jnp.float32),
            pltpu.VMEM((3, 3 * channels, channels), jnp.bfloat16),
            pltpu.SemaphoreType.DMA,
        ],
        compiler_params=pltpu.CompilerParams(vmem_limit_bytes=48 * 2**20),
        name="tile_terms",
    )(
        place, pad_one, pad_two, sides, spread, weight.reshape(3, 3 * channels, channels),
        bias[None],
    )
    shape = (tile_cols, width, group, channels ** (-0.5))
    summed, corr = sum_everywhere(terms, scores, shape)
    grad_weight, grad_bias = pl.pallas_call(
        spread_kernel,
        out_shape=[
            jax.ShapeDtypeStruct((9 * channels, channels), jnp.float32),
            jax.ShapeDtypeStruct((1, channels), jnp.float32),
        ],
        in_specs=[whole],
        out_specs=[whole] * 2,
        compiler_params=pltpu.CompilerParams(vmem_limit_bytes=32 * 2**20),
        name="spread_sum",
    )(summed)
    return (
        corr.reshape(1, side * side, tile_rows, tile_cols),
        grad_weight.reshape(weight.shape),
        grad_bias[0],
    )


def solution(mesh):
    return jax.shard_map(
        shards,
        mesh=mesh,
        in_specs=(
            P("pair", None, "row", "col", None),
            P("pair", None, None, None),
            P(),
            P(),
            P("pair", None, "row", "col"),
        ),
        out_specs=(P("pair", None, "row", "col"), P(), P()),
        check_vma=False,
    )
```

```python
import functools

import jax
import jax.numpy as jnp
from jax import lax
from jax.experimental import pallas as pl
from jax.experimental.pallas import tpu as pltpu
from jax.sharding import PartitionSpec as P

BLK = 32
RAD = 4
MAXOFF = 8
MESH = pl.DeviceIdType.MESH


def skew(cells, period, back):
    lanes = cells.shape[1]
    line = lax.rem(lax.broadcasted_iota(jnp.int32, cells.shape, 0), period)
    step = 1
    while step < period:
        moved = pltpu.roll(cells, lanes - step if back else step, 1)
        cells = jnp.where((line // step) % 2 == 1, moved, cells)
        step *= 2
    return cells


def band_places(width, lanes):
    side = 2 * RAD + 1
    shape = (side * side, lanes)
    band = lax.broadcasted_iota(jnp.int32, shape, 0)
    lane = lax.broadcasted_iota(jnp.int32, shape, 1)
    found = jnp.zeros(shape, jnp.float32)
    for line in range(side):
        first = line * width
        here = (lane - band == line * (width - side)) & (lane >= first) & (lane < first + side)
        found = jnp.where(here, 1.0, found)
    return found


def exchange_plan():
    sizes = {axis: lax.axis_size(axis) for axis in ("row", "col")}
    bits = {
        axis: [1 << place for place in range(size.bit_length() - 1)]
        for axis, size in sizes.items()
    }
    near = [("row", stride) for stride in bits["row"][:1]]
    rest = [("row", stride) for stride in bits["row"][1:]]
    side = [("col", stride) for stride in reversed(bits["col"])]
    return [near + rest + side, near + side + rest]


def sum_kernel(
    plans, runs, shape, terms, scores, total, corr,
    acc, send_half, recv_half, recv_wide, *sems,
):
    rs_send, rs_recv, ag_send, ag_recv, far_send, far_recv = sems
    count = len(plans[0])
    parts = range(len(runs))
    depth = lax.axis_size("pair")
    me = lax.axis_index("pair")

    def partner(step):
        axis, stride = step
        at = lax.axis_index(axis)
        bit = lax.rem(at // stride, 2)
        return bit, {axis: at + stride - 2 * stride * bit}

    def peer(hop):
        return lax.rem(me + hop, depth)

    barrier = pltpu.get_barrier_semaphore()
    for step in plans[0]:
        pl.semaphore_signal(barrier, inc=1, device_id=partner(step)[1], device_id_type=MESH)
    for hop in range(1, depth):
        pl.semaphore_signal(barrier, inc=1, device_id={"pair": peer(hop)}, device_id_type=MESH)
    pl.semaphore_wait(barrier, count + depth - 1)

    tile_cols, width, group, inv_root = shape
    chunk = group * tile_cols
    places = band_places(width, scores.shape[1]).astype(jnp.bfloat16)
    blocks = list(range(scores.shape[0] // chunk))

    def take_band():
        if not blocks:
            return
        at = slice(blocks[0] * chunk, (blocks[0] + 1) * chunk)
        bands = (skew(scores[at, :], tile_cols, True) * inv_root).astype(jnp.bfloat16)
        corr[at, :] = lax.dot_general(
            bands, places, (((1,), (1,)), ((), ())), preferred_element_type=jnp.float32
        ).astype(jnp.bfloat16)
        blocks.pop(0)

    base = [start for _, start, _ in runs]
    trail = [[] for _ in parts]
    waiting = [None for _ in parts]
    sent = []

    def send(src, dst, send_sem, recv_sem, device):
        copy = pltpu.make_async_remote_copy(
            src_ref=src,
            dst_ref=dst,
            send_sem=send_sem,
            recv_sem=recv_sem,
            device_id=device,
            device_id_type=MESH,
        )
        copy.start()
        sent.append(copy)
        return copy

    def absorb(part, place):
        half, _, rows = runs[part]
        size = rows >> (place + 1)
        copy, keep, came = waiting[part]
        copy.wait_recv()
        source = terms if place == 0 else acc
        acc[half, pl.ds(keep, size), :] = source[half, pl.ds(keep, size), :] + came[...].astype(
            jnp.float32
        )
        base[part] = keep

    for place in range(count):
        for part in parts:
            half, start, rows = runs[part]
            size = rows >> (place + 1)
            slot = start + rows - (rows >> place)
            if place > 0:
                absorb(part, place - 1)
            bit, device = partner(plans[half][place])
            keep = pl.multiple_of(base[part] + bit * size, 16)
            give = pl.multiple_of(base[part] + (1 - bit) * size, 16)
            if place == 0:
                src = terms.at[half, pl.ds(give, size), :]
                dst = recv_wide.at[half, pl.ds(start // 2, size), :]
            else:
                send_half[half, slot : slot + size, :] = acc[half, pl.ds(give, size), :].astype(
                    jnp.bfloat16
                )
                src = send_half.at[half, pl.ds(slot, size), :]
                dst = recv_half.at[half, pl.ds(slot, size), :]
            copy = send(src, dst, rs_send.at[part, place], rs_recv.at[part, place], device)
            waiting[part] = (copy, keep, dst)
            trail[part].append(base[part])
        take_band()

    arrivals = [[] for _ in parts]
    for part in parts:
        half, start, rows = runs[part]
        absorb(part, count - 1)
        size = (rows >> count) // depth
        slot = start + rows - (rows >> count)
        for hop in range(1, depth):
            give = pl.multiple_of(base[part] + peer(hop) * size, 16)
            first = slot + (hop - 1) * size
            send_half[half, first : first + size, :] = acc[half, pl.ds(give, size), :].astype(
                jnp.bfloat16
            )
            src = send_half.at[half, pl.ds(first, size), :]
            dst = recv_half.at[half, pl.ds(first, size), :]
            copy = send(
                src, dst, far_send.at[part, hop], far_recv.at[part, hop], {"pair": peer(hop)}
            )
            arrivals[part].append((copy, dst))
    take_band()
    for part in parts:
        half, start, rows = runs[part]
        size = (rows >> count) // depth
        own = pl.ds(pl.multiple_of(base[part] + me * size, 16), size)
        value = acc[half, own, :]
        for copy, came in arrivals[part]:
            copy.wait_recv()
            value = value + came[...].astype(jnp.float32)
        total[half, own, :] = value.astype(jnp.bfloat16)
        block = total.at[half, own, :]
        arrivals[part] = [
            send(
                block,
                block,
                far_send.at[part, depth - 1 + hop],
                far_recv.at[part, depth - 1 + hop],
                {"pair": peer(hop)},
            )
            for hop in range(1, depth)
        ]
    for place in reversed(range(count)):
        for part in parts:
            half, start, rows = runs[part]
            size = rows >> (place + 1)
            for copy in arrivals[part]:
                copy.wait_recv()
            block = total.at[half, pl.ds(pl.multiple_of(base[part], 16), size), :]
            copy = send(
                block,
                block,
                ag_send.at[part, place],
                ag_recv.at[part, place],
                partner(plans[half][place])[1],
            )
            arrivals[part] = [copy]
            base[part] = trail[part][place]
        take_band()
    while blocks:
        take_band()
    for part in parts:
        for copy in arrivals[part]:
            copy.wait_recv()
    for copy in sent:
        copy.wait_send()


def padded_rows(rows):
    devices = lax.axis_size("row") * lax.axis_size("col") * lax.axis_size("pair")
    grain = 16 * devices
    return (rows + grain - 1) // grain * grain


def sum_everywhere(terms, scores, shape):
    plans = exchange_plan()
    rows = terms.shape[1]
    grains = rows // padded_rows(1)
    head = (grains + 1) // 2 * padded_rows(1)
    runs = [(half, 0, head) for half in range(2)]
    if head < rows:
        runs += [(half, head, rows - head) for half in range(2)]
    near = pltpu.SemaphoreType.DMA((len(runs), len(plans[0])))
    far = pltpu.SemaphoreType.DMA((len(runs), 2 * lax.axis_size("pair")))
    return pl.pallas_call(
        functools.partial(sum_kernel, plans, runs, shape),
        out_shape=[
            jax.ShapeDtypeStruct(terms.shape, jnp.bfloat16),
            jax.ShapeDtypeStruct((scores.shape[0], (2 * RAD + 1) ** 2), jnp.bfloat16),
        ],
        in_specs=[pl.BlockSpec(memory_space=pltpu.VMEM)] * 2,
        out_specs=[pl.BlockSpec(memory_space=pltpu.VMEM)] * 2,
        scratch_shapes=[
            pltpu.VMEM(terms.shape, jnp.float32),
            pltpu.VMEM(terms.shape, jnp.bfloat16),
            pltpu.VMEM(terms.shape, jnp.bfloat16),
            pltpu.VMEM(terms.shape, jnp.float32),
            near,
            near,
            near,
            near,
            far,
            far,
        ],
        compiler_params=pltpu.CompilerParams(
            collective_id=1, has_side_effects=True, vmem_limit_bytes=20 * 2**20
        ),
        name="sum_everywhere",
    )(terms, scores)


def halo_kernel(
    wide, edge, width, group, frames, cot, pad_one, pad_two, sides, spread,
    cells, send_sem, recv_sem, own_sem,
):
    row, col = lax.axis_index("row"), lax.axis_index("col")
    row_count, col_count = lax.axis_size("row"), lax.axis_size("col")
    tile_rows, tile_cols = frames.shape[1], frames.shape[2]
    ways = [(down, right) for down in (0, -1, 1) for right in (0, -1, 1) if (down, right) != (0, 0)]

    def lies(down, right):
        inside_rows = (row + down >= 0) & (row + down < row_count)
        inside_cols = (col + right >= 0) & (col + right < col_count)
        return inside_rows & inside_cols

    def device(down, right):
        return {"row": row + down, "col": col + right}

    def span(step, size, halo):
        if step == 0:
            return pl.ds(0, size), pl.ds(halo, size)
        if step > 0:
            return pl.ds(size - halo, halo), pl.ds(0, halo)
        return pl.ds(0, halo), pl.ds(halo + size, halo)

    barrier = pltpu.get_barrier_semaphore()
    for way in ways:
        @pl.when(lies(*way))
        def _():
            pl.semaphore_signal(barrier, inc=1, device_id=device(*way), device_id_type=MESH)
    first = frames[0, :, :edge, :].astype(jnp.float32)
    cells[0] = first[:, 0, :].astype(jnp.bfloat16)
    final = frames[0, :, tile_cols - edge :, :].astype(jnp.float32)
    cells[1] = final[:, edge - 1, :].astype(jnp.bfloat16)
    own = []
    for frame, (pad, halo) in enumerate(((pad_one, 1), (pad_two, wide))):
        middle = pad.at[pl.ds(halo, tile_rows), pl.ds(edge, tile_cols), :]
        own.append(pltpu.make_async_copy(frames.at[frame], middle, own_sem.at[frame]))
        own[-1].start()
    near_rows = 1 + (row > 0).astype(jnp.int32) + (row < row_count - 1).astype(jnp.int32)
    near_cols = 1 + (col > 0).astype(jnp.int32) + (col < col_count - 1).astype(jnp.int32)
    pl.semaphore_wait(barrier, near_rows * near_cols - 1)
    copies = []
    for place, way in enumerate(ways):
        for frame, (pad, halo) in enumerate(((pad_one, 1), (pad_two, wide))):
            take_rows, put_rows = span(way[0], tile_rows, halo)
            take_cols, put_cols = span(way[1], tile_cols, edge)
            source = frames.at[frame, take_rows, take_cols, :]
            target = pad.at[put_rows, put_cols, :]
            if frame == 0 and way[0] == 0:
                source = cells.at[1 if way[1] > 0 else 0]
                target = sides.at[0 if way[1] > 0 else 1]
            copy = pltpu.make_async_remote_copy(
                src_ref=source,
                dst_ref=target,
                send_sem=send_sem.at[place, frame],
                recv_sem=recv_sem.at[place, frame],
                device_id=device(*way),
                device_id_type=MESH,
            )
            copies.append((way, copy))
            pl.when(lies(*way))(copy.start)
    chunk = group * tile_cols
    places = band_places(width, spread.shape[1]).astype(jnp.bfloat16)
    for block in range(spread.shape[0] // chunk):
        at = slice(block * chunk, (block + 1) * chunk)
        bands = jnp.dot(cot[at, :], places, preferred_element_type=jnp.float32)
        spread[at, :] = skew(bands, tile_cols, False).astype(jnp.bfloat16)
    for copy in own:
        copy.wait()
    for way, copy in copies:
        pl.when(lies(-way[0], -way[1]))(copy.wait_recv)
    for way, copy in copies:
        pl.when(lies(*way))(copy.wait_send)


def gather_halos(frames, cot, wide, edge, width, group, lanes):
    tile_rows, tile_cols, channels = frames.shape[1:]
    pads = [
        jax.ShapeDtypeStruct((tile_rows + 2 * halo, tile_cols + 2 * edge, channels), frames.dtype)
        for halo in (1, wide)
    ]
    pads.append(jax.ShapeDtypeStruct((2, tile_rows, channels), frames.dtype))
    pads.append(jax.ShapeDtypeStruct((cot.shape[0], lanes), cot.dtype))
    whole = pl.BlockSpec(memory_space=pltpu.VMEM)
    return pl.pallas_call(
        functools.partial(halo_kernel, wide, edge, width, group),
        out_shape=pads,
        in_specs=[whole] * 2,
        out_specs=[whole] * 4,
        scratch_shapes=[
            pltpu.VMEM((2, tile_rows, channels), frames.dtype),
            pltpu.SemaphoreType.DMA((8, 2)),
            pltpu.SemaphoreType.DMA((8, 2)),
            pltpu.SemaphoreType.DMA((2,)),
        ],
        compiler_params=pltpu.CompilerParams(
            collective_id=0, has_side_effects=True, vmem_limit_bytes=16 * 2**20
        ),
        name="gather_halos",
    )(frames, cot)


def tile_kernel(
    geometry, place, pad_one, pad_two, sides, spread_all, weight_far, bias, scores, terms,
    taps_one, taps_two, pre_one, pre_two, feat_one, feat_two, delta_one, flip_one, flip_two,
    grad_two, sides_wide, weight, weight_sem,
):
    tile_rows, tile_cols, image_rows, image_cols, edge, width, group = geometry
    channels = bias.shape[1]
    load = pltpu.make_async_copy(weight_far, weight, weight_sem)
    load.start()
    lanes = spread_all.shape[1]
    padded_cols = tile_cols + 2 * edge
    window_rows = tile_rows + 2 * RAD
    pixels_two = window_rows * width
    shift_row, shift_col, row_start, col_start = place[0], place[1], place[2], place[3]
    inv_root = channels ** (-0.5)

    across = lax.broadcasted_iota(jnp.int32, (padded_cols, channels), 0) + (col_start - edge)
    inside_cols = (across >= 0) & (across < image_cols)

    def masked(line, image_row):
        inside = inside_cols & (image_row >= 0) & (image_row < image_rows)
        return jnp.where(inside, line.astype(jnp.float32), 0.0)

    sides_wide[:, :8, :] = jnp.zeros_like(sides_wide[:, :8, :])
    sides_wide[:, 8 : 8 + tile_rows, :] = sides[...].astype(jnp.float32)
    sides_wide[:, 8 + tile_rows :, :] = jnp.zeros_like(sides_wide[:, 8 + tile_rows :, :])
    spot = across - (col_start - edge)

    @pl.loop(0, tile_rows + 2, unroll=2)
    def _(line):
        cells = pad_one[line].astype(jnp.float32)
        middle = (line > 0) & (line < tile_rows + 1)
        for end, column in enumerate((edge - 1, edge + tile_cols)):
            side_line = sides_wide[end, pl.ds(line + 7, 1), :]
            cells = jnp.where((spot == column) & middle, side_line, cells)
        cells = masked(cells, row_start - 1 + line)
        for tap in range(3):
            first = edge - 1 + tap
            taps_one[pl.ds(pl.multiple_of(line * tile_cols, 16), tile_cols),
                     tap * channels : (tap + 1) * channels] = (
                cells[first : first + tile_cols].astype(jnp.bfloat16)
            )

    @pl.loop(0, window_rows + 2, unroll=2)
    def _(line):
        at = shift_row + MAXOFF + line
        cells = masked(pad_two[at], row_start - (MAXOFF + RAD + 1) + at)
        cells = pltpu.roll(cells, padded_cols - (shift_col + edge - RAD - 1), 0)
        for tap in range(3):
            taps_two[pl.ds(pl.multiple_of(line * width, 16), width),
                     tap * channels : (tap + 1) * channels] = (
                cells[tap : tap + width].astype(jnp.bfloat16)
            )

    def convolved(taps, first, size, pitch):
        total = jnp.broadcast_to(bias[...], (size, channels))
        for tap in range(3):
            total = total + jnp.dot(
                taps[pl.ds(pl.multiple_of(first + tap * pitch, 16), size), :],
                weight[tap],
                preferred_element_type=jnp.float32,
            )
        return total

    load.wait()
    size_one = group * tile_cols

    @pl.loop(0, tile_rows // group)
    def _(block):
        first = pl.multiple_of(block * size_one, 16)
        pre = convolved(taps_one, first, size_one, tile_cols)
        pre_one[pl.ds(first, size_one), :] = pre
        feat_one[pl.ds(first, size_one), :] = jnp.maximum(pre, 0.0).astype(jnp.bfloat16)

    size_two = group * width

    @pl.loop(0, window_rows // group, unroll=2)
    def _(block):
        first = pl.multiple_of(block * size_two, 16)
        pre = convolved(taps_two, first, size_two, width).reshape(group, width, channels)
        rows = lax.broadcasted_iota(jnp.int32, pre.shape, 0) + (
            row_start + shift_row - RAD + block * group
        )
        cols = lax.broadcasted_iota(jnp.int32, pre.shape, 1) + (col_start + shift_col - RAD)
        inside = (rows >= 0) & (rows < image_rows) & (cols >= 0) & (cols < image_cols)
        pre = jnp.where(inside, pre, 0.0).reshape(size_two, channels)
        pre_two[pl.ds(first, size_two), :] = pre
        feat_two[pl.ds(first, size_two), :] = jnp.maximum(pre, 0.0).astype(jnp.bfloat16)

    feat_two[pixels_two:, :] = jnp.zeros_like(feat_two[pixels_two:, :])
    grad_two[...] = jnp.zeros_like(grad_two)

    @pl.loop(0, tile_rows // group)
    def _(block):
        for inner in range(group):
            row = block * group + inner
            pixels = pl.ds(pl.multiple_of(row * tile_cols, 16), tile_cols)
            window = pl.ds(pl.multiple_of(row * width, 16), lanes)
            spread = spread_all[pixels, :]
            one, two = feat_one[pixels, :], feat_two[window, :]
            scores[pixels, :] = lax.dot_general(
                one, two, (((1,), (1,)), ((), ())), preferred_element_type=jnp.float32
            )
            grad = jnp.dot(spread, two, preferred_element_type=jnp.float32) * inv_root
            grad = jnp.where(pre_one[pixels, :] > 0, grad, 0.0)
            delta_one[pixels, :] = grad.astype(jnp.bfloat16).astype(jnp.float32)
            grad_two[window, :] += lax.dot_general(
                spread, one, (((0,), (0,)), ((), ())), preferred_element_type=jnp.float32
            )

    delta_two = jnp.where(pre_two[...] > 0, grad_two[:pixels_two, :] * inv_root, 0.0)
    bias_term = jnp.sum(delta_one[...], axis=0, keepdims=True)
    bias_term = bias_term + jnp.sum(delta_two, axis=0, keepdims=True)
    flip_one[...] = delta_one[...].T.astype(jnp.bfloat16)
    flip_two[...] = delta_two.T.astype(jnp.bfloat16)

    half = channels // 2
    pixels_one = tile_rows * tile_cols
    for tap_row in range(3):
        for tap_col in range(3):
            cols = slice(tap_col * channels, (tap_col + 1) * channels)
            first_one, first_two = tap_row * tile_cols, tap_row * width
            term = jnp.dot(
                flip_one[...],
                taps_one[first_one : first_one + pixels_one, cols],
                preferred_element_type=jnp.float32,
            ) + jnp.dot(
                flip_two[...],
                taps_two[first_two : first_two + pixels_two, cols],
                preferred_element_type=jnp.float32,
            )
            term = term.T
            first = (tap_row * 3 + tap_col) * channels
            terms[0, first : first + channels, :] = term[:, :half]
            terms[1, first : first + channels, :] = term[:, half:]
    last = 9 * channels
    rest = terms.shape[1] - last
    filler = lax.broadcasted_iota(jnp.int32, (rest, channels), 0) == 0
    filler = jnp.where(filler, jnp.broadcast_to(bias_term, (rest, channels)), 0.0)
    terms[0, last:, :] = filler[:, :half]
    terms[1, last:, :] = filler[:, half:]


def spread_kernel(summed, grad_weight, grad_bias):
    rows, half = grad_weight.shape[0], summed.shape[2]
    for part in range(2):
        lanes = slice(part * half, (part + 1) * half)
        grad_weight[:, lanes] = summed[part, :rows, :].astype(jnp.float32)
        grad_bias[:, lanes] = summed[part, rows : rows + 16, :].astype(jnp.float32)[:1]


def shards(frames, offsets, weight, bias, cotangent):
    tile_rows, tile_cols, channels = (frames.shape[2], frames.shape[3], frames.shape[4])
    row_start = lax.axis_index("row") * tile_rows
    col_start = lax.axis_index("col") * tile_cols
    image_rows = lax.axis_size("row") * tile_rows
    image_cols = lax.axis_size("col") * tile_cols
    wide = MAXOFF + RAD + 1
    edge = (wide + 15) // 16 * 16
    side = 2 * RAD + 1
    width = (tile_cols + 2 * RAD + 15) // 16 * 16
    lanes = (side * width + 127) // 128 * 128
    window_rows = tile_rows + 2 * RAD
    pixels_one, pixels_two = tile_rows * tile_cols, window_rows * width
    long = max(pixels_two, (tile_rows - 1) * width + lanes)
    shift = offsets[0, row_start // BLK, col_start // BLK]
    place = jnp.concatenate([shift, jnp.stack([row_start, col_start])]).astype(jnp.int32)
    group = 4
    cot = jnp.transpose(cotangent[0], (1, 2, 0)).reshape(pixels_one, side * side)
    pad_one, pad_two, sides, spread = gather_halos(
        frames[0], cot, wide, edge, width, group, lanes
    )
    whole = pl.BlockSpec(memory_space=pltpu.VMEM)
    rows = padded_rows(9 * channels + 1)
    geometry = (tile_rows, tile_cols, image_rows, image_cols, edge, width, group)
    scores, terms = pl.pallas_call(
        functools.partial(tile_kernel, geometry),
        out_shape=[
            jax.ShapeDtypeStruct((pixels_one, lanes), jnp.float32),
            jax.ShapeDtypeStruct((2, rows, channels // 2), jnp.float32),
        ],
        in_specs=[pl.BlockSpec(memory_space=pltpu.SMEM)]
        + [whole] * 4
        + [pl.BlockSpec(memory_space=pl.ANY), whole],
        out_specs=[whole] * 2,
        scratch_shapes=[
            pltpu.VMEM(((tile_rows + 2) * tile_cols, 3 * channels), jnp.bfloat16),
            pltpu.VMEM(((window_rows + 2) * width, 3 * channels), jnp.bfloat16),
            pltpu.VMEM((pixels_one, channels), jnp.float32),
            pltpu.VMEM((pixels_two, channels), jnp.float32),
            pltpu.VMEM((pixels_one, channels), jnp.bfloat16),
            pltpu.VMEM((long, channels), jnp.bfloat16),
            pltpu.VMEM((pixels_one, channels), jnp.float32),
            pltpu.VMEM((channels, pixels_one), jnp.bfloat16),
            pltpu.VMEM((channels, pixels_two), jnp.bfloat16),
            pltpu.VMEM((long, channels), jnp.float32),
            pltpu.VMEM((2, tile_rows + 16, channels), jnp.float32),
            pltpu.VMEM((3, 3 * channels, channels), jnp.bfloat16),
            pltpu.SemaphoreType.DMA,
        ],
        compiler_params=pltpu.CompilerParams(vmem_limit_bytes=24 * 2**20),
        name="tile_terms",
    )(
        place, pad_one, pad_two, sides, spread, weight.reshape(3, 3 * channels, channels),
        bias[None],
    )
    shape = (tile_cols, width, group, channels ** (-0.5))
    summed, corr = sum_everywhere(terms, scores, shape)
    grad_weight, grad_bias = pl.pallas_call(
        spread_kernel,
        out_shape=[
            jax.ShapeDtypeStruct((9 * channels, channels), jnp.float32),
            jax.ShapeDtypeStruct((1, channels), jnp.float32),
        ],
        in_specs=[whole],
        out_specs=[whole] * 2,
        compiler_params=pltpu.CompilerParams(vmem_limit_bytes=12 * 2**20),
        name="spread_sum",
    )(summed)
    return (
        jnp.transpose(corr.reshape(tile_rows, tile_cols, side * side), (2, 0, 1))[None],
        grad_weight.reshape(weight.shape),
        grad_bias[0],
    )


def solution(mesh):
    return jax.shard_map(
        shards,
        mesh=mesh,
        in_specs=(
            P("pair", None, "row", "col", None),
            P("pair", None, None, None),
            P(),
            P(),
            P("pair", None, "row", "col"),
        ),
        out_specs=(P("pair", None, "row", "col"), P(), P()),
        check_vma=False,
    )
```
